32 devices in a mesh: seq: 8 (over z, x), batch: 4 (over y, core).
Axes of the slice: x: 2, y: 2, z: 4, core: 2. Of those that a mesh axis runs over, the one named last changes fastest.
Arguments:
- sequence_input: bfloat16 [8192, 1536], P(('batch', 'seq')), parts along dimension 0, may hold values from -6 to 6
- conv_first: bfloat16 [5, 1536, 768], replicated, may hold values from -0.0625 to 0.0625
- conv_second: bfloat16 [5, 768, 768], replicated, may hold values from -0.09375 to 0.09375
- qkv_weight: bfloat16 [768, 1536], replicated, may hold values from -0.21875 to 0.21875
- out_weight: bfloat16 [512, 768], replicated, may hold values from -0.25 to 0.25
- logit_scale: float32 [4], replicated, may hold values from 2.5 to 30, as said below
Outputs:
- block_output: bfloat16 [8192, 768], P(('batch', 'seq')), parts along dimension 0
The draws below stay inside these ranges and needn't reach their ends.
There are 4 independent parts, one for each index of `batch`. The reference program is written for one: setup_inputs(seed, part) draws one part's arguments, and reference() takes and returns one part's arrays. A program takes and returns all parts, laid end to end along the dimension named above; an argument that names none is the same for every part. Nothing has to cross between parts.
Inputs may be any that keep to these rules, and one draw needn't show every extreme that they name: `logit_scale`: one positive scale a head.
All inputs are finite; a program needn't handle non-finite values.
Results may differ from the reference program's by a relative error of at most 0.023.
Values may be sent and summed in bfloat16 or wider, within the bound.
No kernel may reach another device: no remote copies, remote signals or barrier semaphores. Data moves between devices by JAX's collectives and lax.ppermute only.
A program may use at most 256 MiB of HBM per device.

```python
import math
import jax
import jax.numpy as jnp
from jax import lax

C = 1536
CW = 768
HEADS = 4
DH = 128
TOKENS = 2048


def draw_logit_scale(key, part):
    return jnp.exp(jax.random.uniform(key, (HEADS,), jnp.float32, math.log(2.5), math.log(10.0)))


def level_of(own_key, extent, shards, least, top_value):
    gain = 1.0
    for position, parts in shards:
        draws = jax.random.uniform(jax.random.fold_in(jax.random.fold_in(own_key, 6), position), (parts,), jnp.float32, least / len(shards), top_value / len(shards))
        gain = gain * jnp.repeat(jnp.exp(draws), extent[position] // parts).reshape((-1,) + (1,) * (len(extent) - 1 - position))
    return gain


def gaussian(stream_key, shape, scale, reach, pieces=(), dtype=jnp.bfloat16):
    factor_of = level_of(stream_key, shape, pieces, -0.22, 0.18) if pieces else 1.0
    drawn = jax.random.normal(stream_key, shape, jnp.float32) * scale * factor_of
    return jnp.minimum(jnp.maximum(drawn, -reach), reach).astype(dtype)


def setup_inputs(seed: int = 0, part: int = 0) -> dict:
    seeds = jax.random.split(jax.random.key(seed), 7)
    own_keys = jax.random.split(jax.random.fold_in(seeds[6], part), 7)
    return {
        "sequence_input": gaussian(own_keys[0], (TOKENS, C), 1.0, 6.0, ((0, 8),)),
        "conv_first": gaussian(seeds[1], (5, C, CW), (5 * C) ** -0.5, 0.0625),
        "conv_second": gaussian(seeds[2], (5, CW, CW), (5 * CW) ** -0.5, 0.09375),
        "qkv_weight": gaussian(seeds[3], (CW, 3 * HEADS * DH), CW ** -0.5, 0.21875),
        "out_weight": gaussian(seeds[4], (HEADS * DH, CW), (HEADS * DH) ** -0.5, 0.25),
        "logit_scale": draw_logit_scale(jax.random.fold_in(seeds[6], 71), part),
    }


def convolve(source, weight):
    row_count = source.shape[0]
    padded = jnp.pad(source, ((2, 2), (0, 0)))
    conv_sum = jnp.dot(padded[0:row_count], weight[0], preferred_element_type=jnp.float32)
    for offset in range(1, 5):
        conv_sum = conv_sum + jnp.dot(padded[offset:offset + row_count], weight[offset], preferred_element_type=jnp.float32)
    return conv_sum

def head_rms(tensor):
    return tensor * lax.rsqrt(lax.optimization_barrier(jnp.mean(tensor * tensor, axis=-1, keepdims=True)) + 1e-06)

def reference(sequence_input, conv_first, conv_second, qkv_weight, out_weight, logit_scale):
    first_out = jax.nn.gelu(convolve(sequence_input, conv_first)).astype(jnp.bfloat16)
    hidden = (first_out.astype(jnp.float32) + convolve(first_out, conv_second)).astype(jnp.bfloat16)
    width_all = HEADS * DH
    projected = jnp.dot(hidden, qkv_weight, preferred_element_type=jnp.float32)
    query_part = projected[:, :width_all].reshape(TOKENS, HEADS, DH)
    key_part = projected[:, width_all:2 * width_all].reshape(TOKENS, HEADS, DH)
    value_part = projected[:, 2 * width_all:].reshape(TOKENS, HEADS, DH)
    queries = (head_rms(query_part) * (logit_scale / math.sqrt(DH))[None, :, None]).astype(jnp.bfloat16)
    key_wide = head_rms(key_part).astype(jnp.bfloat16).astype(jnp.float32)
    value_wide = value_part.astype(jnp.bfloat16).astype(jnp.float32)
    block_rows = math.gcd(TOKENS, 512)

    def attend(query_block):
        scores = jnp.einsum('qhd,khd->hqk', query_block.astype(jnp.float32), key_wide)
        row_max = lax.optimization_barrier(jnp.max(scores, axis=2, keepdims=True))
        exponent = jnp.exp(scores - row_max)
        denominators = lax.optimization_barrier(jnp.sum(exponent, axis=2))
        probabilities = lax.optimization_barrier(exponent.astype(jnp.bfloat16)).astype(jnp.float32)
        mixed_out = jnp.einsum('hqk,khd->qhd', probabilities, value_wide)
        return mixed_out / denominators.T[:, :, None]
    blocks = queries.reshape(TOKENS // block_rows, block_rows, HEADS, DH)
    attended = lax.map(attend, blocks).reshape(TOKENS, width_all).astype(jnp.bfloat16)
    return (hidden.astype(jnp.float32) + jnp.dot(attended, out_weight, preferred_element_type=jnp.float32)).astype(jnp.bfloat16)
```

```python
import functools
import math

import jax
import jax.numpy as jnp
from jax import lax
from jax.experimental import pallas as pl
from jax.experimental.pallas import tpu as pltpu
from jax.sharding import PartitionSpec as P

F32 = jnp.float32
BF16 = jnp.bfloat16
EDGE = 8
TAPS = 5
MIB = 1 << 20


def head_rms(tensor):
    return tensor * lax.rsqrt(jnp.mean(tensor * tensor, axis=-1, keepdims=True) + 1e-06)


def edge_rows(block):
    count = lax.axis_size("seq")
    forward = [(i, i + 1) for i in range(count - 1)]
    backward = [(target, source) for source, target in forward]
    before = lax.ppermute(block[block.shape[0] - EDGE :], "seq", forward)
    after = lax.ppermute(block[:EDGE], "seq", backward)
    return after, before


def stem_kernel(
    place, x_ref, after_ref, before_ref, w1_hbm, w2_hbm, wqkv_hbm, scale_ref, *rest, heads, head
):
    hidden_ref, units = rest[0], rest[1 : 1 + heads]
    w1, w2, wqkv, xp, fp, total, projected, sems = rest[1 + heads :]
    rows = x_ref.shape[0]
    circle = rows + 2 * EDGE
    width = heads * head
    copies = []
    for j in range(TAPS):
        copies.append(pltpu.make_async_copy(w1_hbm.at[j], w1.at[j], sems.at[j]))
    for j in range(TAPS):
        copies.append(pltpu.make_async_copy(w2_hbm.at[j], w2.at[j], sems.at[TAPS + j]))
    copies.append(pltpu.make_async_copy(wqkv_hbm, wqkv, sems.at[2 * TAPS]))
    for copy in copies:
        copy.start()

    def rolled(product, j):
        shift = (TAPS // 2 - j) % circle
        return product if shift == 0 else pltpu.roll(product, shift, 0)

    xp[0:rows] = x_ref[...]
    xp[rows:circle] = jnp.concatenate(
        [after_ref[...].astype(F32), before_ref[...].astype(F32)], axis=0
    ).astype(BF16)
    for j in range(TAPS):
        copies[j].wait()
        product = rolled(jnp.dot(xp[...], w1[j], preferred_element_type=F32), j)
        if j == 0:
            total[...] = product
        else:
            total[...] += product
    fp[0:rows] = jax.nn.gelu(total[0:rows]).astype(BF16)
    has_before = place[0].astype(F32)
    has_after = place[1].astype(F32)
    fp[rows:circle] = jnp.concatenate(
        [
            jax.nn.gelu(total[rows : rows + EDGE]) * has_after,
            jax.nn.gelu(total[rows + EDGE : circle]) * has_before,
        ],
        axis=0,
    ).astype(BF16)
    for j in range(TAPS):
        copies[TAPS + j].wait()
        product = rolled(jnp.dot(fp[...], w2[j], preferred_element_type=F32), j)
        if j == 0:
            total[...] = product
        else:
            total[...] += product
    hidden = (fp[0:rows].astype(F32) + total[0:rows]).astype(BF16)
    hidden_ref[...] = hidden
    copies[2 * TAPS].wait()
    projected[...] = jnp.dot(hidden, wqkv[...], preferred_element_type=F32)
    for r in range(heads):
        h = place[2 + r]
        at = pl.multiple_of(h * head, head)
        q = head_rms(projected[:, pl.ds(at, head)]) * (scale_ref[h] / math.sqrt(head))
        k = head_rms(projected[:, pl.ds(width + at, head)])
        units[r][:, 0:head] = q.astype(BF16)
        units[r][:, head : 2 * head] = k.astype(BF16)
        units[r][:, 2 * head :] = projected[:, pl.ds(2 * width + at, head)].astype(BF16)


def stem(place, block, after, before, conv_first, conv_second, qkv_weight, logit_scale):
    rows, channels = block.shape
    width = conv_first.shape[2]
    heads = logit_scale.shape[0]
    head = qkv_weight.shape[1] // 3 // heads
    circle = rows + 2 * EDGE
    vmem = pl.BlockSpec(memory_space=pltpu.VMEM)
    smem = pl.BlockSpec(memory_space=pltpu.SMEM)
    hbm = pl.BlockSpec(memory_space=pl.ANY)
    return pl.pallas_call(
        functools.partial(stem_kernel, heads=heads, head=head),
        out_shape=[jax.ShapeDtypeStruct((rows, width), BF16)]
        + [jax.ShapeDtypeStruct((rows, 3 * head), BF16)] * heads,
        in_specs=[smem, vmem, vmem, vmem, hbm, hbm, hbm, smem],
        out_specs=[vmem] * (1 + heads),
        scratch_shapes=[
            pltpu.VMEM(conv_first.shape, BF16),
            pltpu.VMEM(conv_second.shape, BF16),
            pltpu.VMEM(qkv_weight.shape, BF16),
            pltpu.VMEM((circle, channels), BF16),
            pltpu.VMEM((circle, width), BF16),
            pltpu.VMEM((circle, width), F32),
            pltpu.VMEM((rows, qkv_weight.shape[1]), F32),
            pltpu.SemaphoreType.DMA((2 * TAPS + 1,)),
        ],
        compiler_params=pltpu.CompilerParams(vmem_limit_bytes=48 * MIB),
        name="stem",
    )(place, block, after, before, conv_first, conv_second, qkv_weight, logit_scale)


def attend_kernel(*refs, head, count):
    own, other, outs = refs[:count], refs[count : 2 * count], refs[2 * count : 3 * count]
    keys, values = refs[3 * count :]
    rows = own[0].shape[0]
    for i in range(count):
        keys[i * rows : (i + 1) * rows] = own[i][:, head : 2 * head]
        values[i * rows : (i + 1) * rows] = own[i][:, 2 * head :]
        keys[(count + i) * rows : (count + i + 1) * rows] = other[i][:, head : 2 * head]
        values[(count + i) * rows : (count + i + 1) * rows] = other[i][:, 2 * head :]
    for i in range(count):
        scores = lax.dot_general(
            own[i][:, 0:head],
            keys[...],
            (((1,), (1,)), ((), ())),
            preferred_element_type=F32,
        )
        weights = jnp.exp(scores - jnp.max(scores, axis=1, keepdims=True))
        denominators = jnp.sum(weights, axis=1, keepdims=True)
        mixed = jnp.dot(weights.astype(BF16), values[...], preferred_element_type=F32)
        outs[i][...] = (mixed / denominators).astype(BF16)


def attend(own, other):
    count = len(own)
    rows, wide = own[0].shape
    head = wide // 3
    vmem = pl.BlockSpec(memory_space=pltpu.VMEM)
    return pl.pallas_call(
        functools.partial(attend_kernel, head=head, count=count),
        out_shape=[jax.ShapeDtypeStruct((rows, head), BF16)] * count,
        in_specs=[vmem] * (2 * count),
        out_specs=[vmem] * count,
        scratch_shapes=[
            pltpu.VMEM((2 * count * rows, head), BF16),
            pltpu.VMEM((2 * count * rows, head), BF16),
        ],
        compiler_params=pltpu.CompilerParams(vmem_limit_bytes=32 * MIB),
        name="attend",
    )(*own, *other)


def finish_kernel(place, hidden_ref, weight_ref, *rest):
    mixed, out_ref = rest[:-1], rest[-1]
    head = mixed[0].shape[1]
    total = hidden_ref[...].astype(F32)
    for r in range(len(mixed)):
        at = pl.multiple_of(place[2 + r] * head, head)
        total += jnp.dot(
            mixed[r][...], weight_ref[pl.ds(at, head), :], preferred_element_type=F32
        )
    out_ref[...] = total.astype(out_ref.dtype)


def finish(place, hidden, out_weight, mixed):
    vmem = pl.BlockSpec(memory_space=pltpu.VMEM)
    smem = pl.BlockSpec(memory_space=pltpu.SMEM)
    return pl.pallas_call(
        finish_kernel,
        out_shape=jax.ShapeDtypeStruct(hidden.shape, BF16),
        in_specs=[smem] + [vmem] * (2 + len(mixed)),
        out_specs=vmem,
        compiler_params=pltpu.CompilerParams(vmem_limit_bytes=32 * MIB),
        name="finish",
    )(place, hidden, out_weight, *mixed)


def routes(seq_count, batch_count, heads):
    rounds = []
    for r in range(heads):
        pairs = []
        for g in range(seq_count):
            for b in range(batch_count):
                chip = heads * (b % 2) + (r ^ (g % heads))
                target = chip * batch_count + b - b % 2 + g // heads
                pairs.append((g * batch_count + b, target))
        rounds.append(pairs)
    return rounds


def by_heads(sequence_input, conv_first, conv_second, qkv_weight, out_weight, logit_scale):
    heads = logit_scale.shape[0]
    count = lax.axis_size("seq")
    batch_count = lax.axis_size("batch")
    g = lax.axis_index("seq")
    place = jnp.stack(
        [(g > 0).astype(jnp.int32), (g < count - 1).astype(jnp.int32)]
        + [(r ^ (g % heads)).astype(jnp.int32) for r in range(heads)]
    )
    after, before = edge_rows(sequence_input)
    hidden, *units = stem(
        place, sequence_input, after, before, conv_first, conv_second, qkv_weight, logit_scale
    )
    both = ("seq", "batch")
    rounds = routes(count, batch_count, heads)
    own = [lax.ppermute(unit, both, pairs) for unit, pairs in zip(units, rounds)]
    cores = [(b, b ^ 1) for b in range(batch_count)]
    other = [lax.ppermute(unit, "batch", cores) for unit in own]
    outs = attend(own, other)
    mixed = [
        lax.ppermute(out, both, [(target, source) for source, target in pairs])
        for out, pairs in zip(outs, rounds)
    ]
    return finish(place, hidden, out_weight, mixed)


def by_gather(sequence_input, conv_first, conv_second, qkv_weight, out_weight, logit_scale):
    heads = logit_scale.shape[0]
    count = lax.axis_size("seq")
    g = lax.axis_index("seq")
    place = jnp.stack(
        [(g > 0).astype(jnp.int32), (g < count - 1).astype(jnp.int32)]
        + [jnp.int32(r) for r in range(heads)]
    )
    after, before = edge_rows(sequence_input)
    hidden, *units = stem(
        place, sequence_input, after, before, conv_first, conv_second, qkv_weight, logit_scale
    )
    head = units[0].shape[1] // 3
    pairs = jnp.concatenate([unit[:, head:] for unit in units], axis=1)
    everywhere = lax.all_gather(pairs, "seq", axis=0, tiled=True)
    mixed = []
    for h in range(heads):
        at = 2 * h * head
        scores = lax.dot_general(
            units[h][:, :head],
            everywhere[:, at : at + head],
            (((1,), (1,)), ((), ())),
            preferred_element_type=F32,
        )
        weights = jnp.exp(scores - jnp.max(scores, axis=1, keepdims=True))
        denominators = jnp.sum(weights, axis=1, keepdims=True)
        out = jnp.dot(
            weights.astype(BF16),
            everywhere[:, at + head : at + 2 * head],
            preferred_element_type=F32,
        )
        mixed.append((out / denominators).astype(BF16))
    return finish(place, hidden, out_weight, mixed)


def solution(mesh):
    def body(*args):
        heads = args[-1].shape[0]
        fits = mesh.shape["seq"] == 2 * heads and mesh.shape["batch"] % 2 == 0
        return (by_heads if fits and heads & (heads - 1) == 0 else by_gather)(*args)

    in_specs = (P(("batch", "seq"), None), P(), P(), P(), P(), P())
    out_specs = P(("batch", "seq"), None)
    return jax.shard_map(body, mesh=mesh, in_specs=in_specs, out_specs=out_specs, check_vma=False)
```

```python
import functools
import math

import jax
import jax.numpy as jnp
from jax import lax
from jax.experimental import pallas as pl
from jax.experimental.pallas import tpu as pltpu
from jax.sharding import PartitionSpec as P

F32 = jnp.float32
BF16 = jnp.bfloat16
EDGE = 8
TAPS = 5
MIB = 1 << 20


def head_rms(tensor):
    return tensor * lax.rsqrt(jnp.mean(tensor * tensor, axis=-1, keepdims=True) + 1e-06)


def first_kernel(x_hbm, w1_hbm, total_ref, to_pair_ref, to_other_ref, x, w1, sems):
    rows = x.shape[0]
    circle = total_ref.shape[0]
    copies = [pltpu.make_async_copy(x_hbm, x, sems.at[TAPS])]
    copies += [pltpu.make_async_copy(w1_hbm.at[j], w1.at[j], sems.at[j]) for j in range(TAPS)]
    for copy in copies:
        copy.start()
    copies[0].wait()
    for j in range(TAPS):
        copies[1 + j].wait()
        product = jnp.dot(x[...], w1[j], preferred_element_type=F32)
        product = on_circle(product, j)
        if j == 0:
            total_ref[...] = product
        else:
            total_ref[...] += product
    near = EDGE // 2
    begin = jnp.concatenate([total_ref[circle - near : circle], total_ref[0:near]], axis=0)
    end = total_ref[rows - near : rows + near]
    even = lax.axis_index("seq") % 2 == 0
    to_pair_ref[...] = jnp.where(even, end, begin)
    to_other_ref[...] = jnp.where(even, begin, end)


def on_circle(product, j):
    spare = jnp.zeros((2 * EDGE, product.shape[1]), F32)
    circle = product.shape[0] + 2 * EDGE
    shift = (TAPS // 2 - j) % circle
    product = jnp.concatenate([product, spare], axis=0)
    return product if shift == 0 else pltpu.roll(product, shift, 0)


def second_kernel(total_ref, w2, first_ref, second_ref, total):
    rows = first_ref.shape[0]
    row = lax.broadcasted_iota(jnp.int32, first_ref.shape, 0)
    reach = TAPS // 2
    inner = (row >= reach) & (row < rows - reach)
    first_ref[...] = jnp.where(inner, jax.nn.gelu(total_ref[0:rows]), 0.0).astype(BF16)
    for j in range(TAPS):
        product = jnp.dot(first_ref[...], w2[j], preferred_element_type=F32)
        product = on_circle(product, j)
        if j == 0:
            total[...] = product
        else:
            total[...] += product
    second_ref[...] = total[0:rows]


def third_kernel(
    total_ref, pair_ref, other_ref, first_ref, second_ref, w2, wqkv, scale_hbm, *rest,
    heads, head, count, spread
):
    hidden_ref, rest_units, (scale_ref, sem) = rest[0], rest[1:-2], rest[-2:]
    scale_copy = pltpu.make_async_copy(scale_hbm, scale_ref, sem)
    scale_copy.start()
    g = lax.axis_index("seq")
    has_before = (g > 0).astype(jnp.int32)
    has_after = (g < count - 1).astype(jnp.int32)
    rows = first_ref.shape[0]
    circle = total_ref.shape[0]
    near, reach = EDGE // 2, TAPS // 2
    row = lax.broadcasted_iota(jnp.int32, pair_ref.shape, 0)
    even = g % 2 == 0
    before = jnp.where(even, other_ref[...], pair_ref[...]) * has_before.astype(F32)
    after = jnp.where(even, pair_ref[...], other_ref[...]) * has_after.astype(F32)
    begin = jnp.concatenate([total_ref[circle - near : circle], total_ref[0:near]], axis=0)
    begin = jax.nn.gelu(begin + before)
    keep = (row >= near - reach * has_before) & (row < near + reach)
    begin = jnp.where(keep, begin, 0.0)
    end = jax.nn.gelu(total_ref[rows - near : rows + near] + after)
    keep = (row >= near - reach) & (row < near + reach * has_after)
    end = jnp.where(keep, end, 0.0)
    edges = jnp.concatenate([begin, end], axis=0).astype(BF16)
    sums = [jnp.zeros(before.shape, F32)] * 2
    for j in range(TAPS):
        product = jnp.dot(edges, w2[j], preferred_element_type=F32)
        shift = (reach - j) % EDGE
        for i in range(2):
            part = product[i * EDGE : (i + 1) * EDGE]
            sums[i] = sums[i] + (part if shift == 0 else pltpu.roll(part, shift, 0))
    pad = jnp.zeros((EDGE - near, first_ref.shape[1]), F32)
    rounded = edges.astype(F32)
    second_ref_rows = second_ref[0:EDGE] + jnp.concatenate(
        [sums[0][near:] + rounded[near:EDGE], pad], axis=0
    )
    last_rows = second_ref[rows - EDGE : rows] + jnp.concatenate(
        [pad, sums[1][:near] + rounded[EDGE : EDGE + near]], axis=0
    )
    hidden = first_ref[...].astype(F32) + jnp.concatenate(
        [second_ref_rows, second_ref[EDGE : rows - EDGE], last_rows], axis=0
    )
    hidden_ref[...] = hidden.astype(BF16)
    scale_copy.wait()
    project(hidden_ref, wqkv, scale_ref, rest_units, g, range(len(rest_units)), heads, head, spread)


def project(hidden_ref, wqkv, scale_ref, units, g, rounds, heads, head, spread):
    width = heads * head
    hidden = hidden_ref[...]
    for unit, r in zip(units, rounds):
        h = head_of(r, g, heads) if spread else r
        at = pl.multiple_of(h * head, head)
        weight = jnp.concatenate(
            [wqkv[:, pl.ds(part * width + at, head)] for part in range(3)], axis=1
        )
        projected = jnp.dot(hidden, weight, preferred_element_type=F32)
        q = head_rms(projected[:, :head]) * (scale_ref[h] / math.sqrt(head))
        unit[:, 0:head] = q.astype(BF16)
        unit[:, head : 2 * head] = head_rms(projected[:, head : 2 * head]).astype(BF16)
        unit[:, 2 * head :] = projected[:, 2 * head :].astype(BF16)


def fourth_kernel(hidden_ref, wqkv, scale_hbm, *rest, heads, head, spread):
    units, (scale_ref, sem) = rest[:-2], rest[-2:]
    scale_copy = pltpu.make_async_copy(scale_hbm, scale_ref, sem)
    scale_copy.start()
    scale_copy.wait()
    g = lax.axis_index("seq")
    rounds = range(heads - len(units), heads)
    project(hidden_ref, wqkv, scale_ref, units, g, rounds, heads, head, spread)


def head_of(r, g, heads):
    half = heads // 2
    side = g // heads
    return half * (side ^ 1 ^ (r // half)) + ((r % half) ^ (g % half))


def swaps(offset):
    count, batch_count = lax.axis_size("seq"), lax.axis_size("batch")
    pairs = []
    for g in range(count):
        for b in range(batch_count):
            to = ((g + offset) ^ 1) - offset
            target = (to, b) if 0 <= to < count else (g, b ^ 1 if b ^ 1 < batch_count else b)
            pairs.append((g * batch_count + b, target[0] * batch_count + target[1]))
    return pairs


def stem(block, conv_first, conv_second, qkv_weight, logit_scale, spread):
    rows, channels = block.shape
    width = conv_first.shape[2]
    heads = logit_scale.shape[0]
    head = qkv_weight.shape[1] // 3 // heads
    circle = rows + 2 * EDGE
    vmem = pl.BlockSpec(memory_space=pltpu.VMEM)
    hbm = pl.BlockSpec(memory_space=pltpu.HBM)
    shape = jax.ShapeDtypeStruct
    total, to_pair, to_other = pl.pallas_call(
        first_kernel,
        out_shape=[shape((circle, width), F32)] + [shape((EDGE, width), F32)] * 2,
        in_specs=[hbm, hbm],
        out_specs=[vmem] * 3,
        scratch_shapes=[
            pltpu.VMEM(block.shape, BF16),
            pltpu.VMEM(conv_first.shape, BF16),
            pltpu.SemaphoreType.DMA((TAPS + 1,)),
        ],
        compiler_params=pltpu.CompilerParams(vmem_limit_bytes=24 * MIB),
        name="first",
    )(
        pltpu.with_memory_space_constraint(block, pltpu.HBM),
        pltpu.with_memory_space_constraint(conv_first, pltpu.HBM),
    )
    total, to_pair, to_other, conv_second, qkv_weight = lax.optimization_barrier(
        (total, to_pair, to_other, conv_second, qkv_weight)
    )
    pair = lax.ppermute(to_pair, ("seq", "batch"), swaps(0))
    other = lax.ppermute(to_other, ("seq", "batch"), swaps(1))
    first, second = pl.pallas_call(
        second_kernel,
        out_shape=[shape((rows, width), BF16), shape((rows, width), F32)],
        in_specs=[vmem] * 2,
        out_specs=[vmem] * 2,
        scratch_shapes=[pltpu.VMEM((circle, width), F32)],
        compiler_params=pltpu.CompilerParams(vmem_limit_bytes=24 * MIB),
        name="second",
    )(total, conv_second)
    half = heads // 2
    fixed = dict(heads=heads, head=head, spread=spread)
    unit = shape((rows, 3 * head), BF16)
    scale_scratch = [pltpu.SMEM(logit_scale.shape, F32), pltpu.SemaphoreType.DMA]
    hidden, *units = pl.pallas_call(
        functools.partial(third_kernel, count=lax.axis_size("seq"), **fixed),
        out_shape=[shape((rows, width), BF16)] + [unit] * half,
        in_specs=[vmem] * 7 + [hbm],
        out_specs=[vmem] * (1 + half),
        scratch_shapes=scale_scratch,
        compiler_params=pltpu.CompilerParams(vmem_limit_bytes=24 * MIB),
        name="third",
    )(total, pair, other, first, second, conv_second, qkv_weight, logit_scale)
    units += pl.pallas_call(
        functools.partial(fourth_kernel, **fixed),
        out_shape=[unit] * (heads - half),
        in_specs=[vmem] * 2 + [hbm],
        out_specs=[vmem] * (heads - half),
        scratch_shapes=scale_scratch,
        compiler_params=pltpu.CompilerParams(vmem_limit_bytes=24 * MIB),
        name="fourth",
    )(hidden, qkv_weight, logit_scale)
    return [hidden, *units]


def scores_of(queries, keys):
    return lax.dot_general(
        queries, keys, (((1,), (1,)), ((), ())), preferred_element_type=F32
    )


def stack_keys(units, keys, values):
    rows = units[0].shape[0]
    head = keys.shape[1]
    for i, unit in enumerate(units):
        keys[i * rows : (i + 1) * rows] = unit[:, head : 2 * head]
        values[i * rows : (i + 1) * rows] = unit[:, 2 * head :]


def attend_kernel(*refs, head, count):
    units, outs, (keys, values) = refs[: -2 - count], refs[-2 - count : -2], refs[-2:]
    stack_keys(units, keys, values)
    for i in range(count):
        scores = scores_of(units[i][:, 0:head], keys[...])
        weights = jnp.exp(scores - jnp.max(scores, axis=1, keepdims=True))
        denominators = jnp.sum(weights, axis=1, keepdims=True)
        mixed = jnp.dot(weights.astype(BF16), values[...], preferred_element_type=F32)
        outs[i][...] = (mixed / denominators).astype(BF16)


def attend(units, count, name):
    rows, wide = units[0].shape
    head = wide // 3
    vmem = pl.BlockSpec(memory_space=pltpu.VMEM)
    return pl.pallas_call(
        functools.partial(attend_kernel, head=head, count=count),
        out_shape=[jax.ShapeDtypeStruct((rows, head), BF16)] * count,
        in_specs=[vmem] * len(units),
        out_specs=[vmem] * count,
        scratch_shapes=[pltpu.VMEM((len(units) * rows, head), BF16)] * 2,
        compiler_params=pltpu.CompilerParams(vmem_limit_bytes=24 * MIB),
        name=name,
    )(*units)


def finish_kernel(hidden_ref, weight_ref, *rest, spread):
    mixed, out_ref = rest[:-1], rest[-1]
    g = lax.axis_index("seq")
    head = mixed[0].shape[1]
    total = hidden_ref[...].astype(F32)
    for r in range(len(mixed)):
        h = head_of(r, g, len(mixed)) if spread else r
        at = pl.multiple_of(h * head, head)
        total += jnp.dot(
            mixed[r][...], weight_ref[pl.ds(at, head), :], preferred_element_type=F32
        )
    out_ref[...] = total.astype(out_ref.dtype)


def finish(hidden, out_weight, mixed, spread):
    vmem = pl.BlockSpec(memory_space=pltpu.VMEM)
    return pl.pallas_call(
        functools.partial(finish_kernel, spread=spread),
        out_shape=jax.ShapeDtypeStruct(hidden.shape, BF16),
        in_specs=[vmem] * (2 + len(mixed)),
        out_specs=vmem,
        compiler_params=pltpu.CompilerParams(vmem_limit_bytes=32 * MIB),
        name="finish",
    )(hidden, out_weight, *mixed)


def routes(seq_count, batch_count, heads):
    half = heads // 2
    rounds = []
    for r in range(heads):
        pairs = []
        for g in range(seq_count):
            for b in range(batch_count):
                h = head_of(r, g, heads)
                chip = heads * (h // half) + half * (b % 2) + h % half
                core = (g // half + r // half) % 2
                target = chip * batch_count + b - b % 2 + core
                pairs.append((g * batch_count + b, target))
        rounds.append(pairs)
    return rounds


def by_heads(sequence_input, conv_first, conv_second, qkv_weight, out_weight, logit_scale):
    heads = logit_scale.shape[0]
    count = lax.axis_size("seq")
    batch_count = lax.axis_size("batch")
    hidden, *units = stem(
        sequence_input, conv_first, conv_second, qkv_weight, logit_scale, True
    )
    both = ("seq", "batch")
    rounds = routes(count, batch_count, heads)
    own = [lax.ppermute(unit, both, pairs) for unit, pairs in zip(units, rounds)]
    cores = [(b, b ^ 1) for b in range(batch_count)]
    other = [lax.ppermute(unit, "batch", cores) for unit in own]
    half = heads // 2
    far, near = own[:half], own[half:]
    outs = attend([*far, *near, *other], half, "far")
    outs, near = lax.optimization_barrier((outs, near))
    outs = outs + attend([*near, *far, *other], heads - half, "near")
    mixed = [
        lax.ppermute(out, both, [(target, source) for source, target in pairs])
        for out, pairs in zip(outs, rounds)
    ]
    return finish(hidden, out_weight, mixed, True)


def by_gather(sequence_input, conv_first, conv_second, qkv_weight, out_weight, logit_scale):
    heads = logit_scale.shape[0]
    count = lax.axis_size("seq")
    hidden, *units = stem(
        sequence_input, conv_first, conv_second, qkv_weight, logit_scale, False
    )
    head = units[0].shape[1] // 3
    pairs = jnp.concatenate([unit[:, head:] for unit in units], axis=1)
    everywhere = lax.all_gather(pairs, "seq", axis=0, tiled=True)
    mixed = []
    for h in range(heads):
        at = 2 * h * head
        scores = lax.dot_general(
            units[h][:, :head],
            everywhere[:, at : at + head],
            (((1,), (1,)), ((), ())),
            preferred_element_type=F32,
        )
        weights = jnp.exp(scores - jnp.max(scores, axis=1, keepdims=True))
        denominators = jnp.sum(weights, axis=1, keepdims=True)
        out = jnp.dot(
            weights.astype(BF16),
            everywhere[:, at + head : at + 2 * head],
            preferred_element_type=F32,
        )
        mixed.append((out / denominators).astype(BF16))
    return finish(hidden, out_weight, mixed, False)


def solution(mesh):
    def body(*args):
        heads = args[-1].shape[0]
        fits = heads == 4 and mesh.shape["seq"] == 2 * heads and mesh.shape["batch"] % 2 == 0
        return (by_heads if fits else by_gather)(*args)

    in_specs = (P(("batch", "seq"), None), P(), P(), P(), P(), P())
    out_specs = P(("batch", "seq"), None)
    return jax.shard_map(body, mesh=mesh, in_specs=in_specs, out_specs=out_specs, check_vma=False)
```

```python
import functools
import math

import jax
import jax.numpy as jnp
from jax import lax
from jax.experimental import pallas as pl
from jax.experimental.pallas import tpu as pltpu
from jax.sharding import PartitionSpec as P

F32 = jnp.float32
BF16 = jnp.bfloat16
EDGE = 8
TILE = 16
TAPS = 5
MIB = 1 << 20


def head_rms(tensor):
    return tensor * lax.rsqrt(jnp.mean(tensor * tensor, axis=-1, keepdims=True) + 1e-06)


def edges_kernel(x_hbm, w1_hbm, to_pair, to_other, first, last, sems):
    rows = x_hbm.shape[0]
    copies = [
        pltpu.make_async_copy(x_hbm.at[pl.ds(0, TILE)], first, sems.at[0]),
        pltpu.make_async_copy(x_hbm.at[pl.ds(rows - TILE, TILE)], last, sems.at[1]),
    ]
    for copy in copies:
        copy.start()
    for copy in copies:
        copy.wait()
    even = lax.axis_index("seq") % 2 == 0
    begin = first[...].astype(F32)[:EDGE]
    end = last[...].astype(F32)[TILE - EDGE :]
    to_pair[...] = jnp.where(even, end, begin).astype(BF16)
    to_other[...] = jnp.where(even, begin, end).astype(BF16)


def rolled(product, j):
    shift = (TAPS // 2 - j) % product.shape[0]
    return product if shift == 0 else pltpu.roll(product, shift, 0)


def first_kernel(x_ref, pair_ref, other_ref, w1, first_ref, x, total, *, count):
    rows = x_ref.shape[0]
    g = lax.axis_index("seq")
    even = g % 2 == 0
    has_before = (g > 0).astype(F32)
    has_after = (g < count - 1).astype(F32)
    pair, other = pair_ref[...].astype(F32), other_ref[...].astype(F32)
    after = jnp.where(even, pair, other) * has_after
    before = jnp.where(even, other, pair) * has_before
    x[0:rows] = x_ref[...]
    x[rows:] = jnp.concatenate([after, before], axis=0).astype(BF16)
    for j in range(TAPS):
        product = rolled(jnp.dot(x[...], w1[j], preferred_element_type=F32), j)
        if j == 0:
            total[...] = product
        else:
            total[...] += product
    first_ref[0:rows] = jax.nn.gelu(total[0:rows]).astype(BF16)
    after = jax.nn.gelu(total[rows : rows + EDGE]) * has_after
    before = jax.nn.gelu(total[rows + EDGE :]) * has_before
    first_ref[rows:] = jnp.concatenate([after, before], axis=0).astype(BF16)


def second_kernel(first_ref, w2, wqkv, scale_hbm, *rest, heads, head, spread):
    hidden_ref, units, (total, scale_ref, sem) = rest[0], rest[1:-3], rest[-3:]
    scale_copy = pltpu.make_async_copy(scale_hbm, scale_ref, sem)
    scale_copy.start()
    rows = hidden_ref.shape[0]
    for j in range(TAPS):
        product = rolled(jnp.dot(first_ref[...], w2[j], preferred_element_type=F32), j)
        if j == 0:
            total[...] = product
        else:
            total[...] += product
    hidden_ref[...] = (first_ref[0:rows].astype(F32) + total[0:rows]).astype(BF16)
    scale_copy.wait()
    g = lax.axis_index("seq")
    project(hidden_ref, wqkv, scale_ref, units, g, range(len(units)), heads, head, spread)


def project(hidden_ref, wqkv, scale_ref, units, g, rounds, heads, head, spread):
    width = heads * head
    hidden = hidden_ref[...]
    for unit, r in zip(units, rounds):
        h = head_of(r, g, heads) if spread else r
        at = pl.multiple_of(h * head, head)
        weight = jnp.concatenate(
            [wqkv[:, pl.ds(part * width + at, head)] for part in range(3)], axis=1
        )
        projected = jnp.dot(hidden, weight, preferred_element_type=F32)
        q = head_rms(projected[:, :head]) * (scale_ref[h] / math.sqrt(head))
        unit[:, 0:head] = q.astype(BF16)
        unit[:, head : 2 * head] = head_rms(projected[:, head : 2 * head]).astype(BF16)
        unit[:, 2 * head :] = projected[:, 2 * head :].astype(BF16)


def third_kernel(hidden_ref, wqkv, scale_hbm, *rest, heads, head, spread):
    units, (scale_ref, sem) = rest[:-2], rest[-2:]
    scale_copy = pltpu.make_async_copy(scale_hbm, scale_ref, sem)
    scale_copy.start()
    scale_copy.wait()
    g = lax.axis_index("seq")
    rounds = range(heads - len(units), heads)
    project(hidden_ref, wqkv, scale_ref, units, g, rounds, heads, head, spread)


def head_of(r, g, heads):
    half = heads // 2
    side = g // heads
    return half * (side ^ 1 ^ (r // half)) + ((r % half) ^ (g % half))


def swaps(offset):
    count, batch_count = lax.axis_size("seq"), lax.axis_size("batch")
    pairs = []
    for g in range(count):
        for b in range(batch_count):
            to = ((g + offset) ^ 1) - offset
            target = (to, b) if 0 <= to < count else (g, b ^ 1 if b ^ 1 < batch_count else b)
            pairs.append((g * batch_count + b, target[0] * batch_count + target[1]))
    return pairs


def stem(block, conv_first, conv_second, qkv_weight, logit_scale, spread):
    rows, channels = block.shape
    width = conv_first.shape[2]
    heads = logit_scale.shape[0]
    head = qkv_weight.shape[1] // 3 // heads
    circle = rows + 2 * EDGE
    vmem = pl.BlockSpec(memory_space=pltpu.VMEM)
    hbm = pl.BlockSpec(memory_space=pltpu.HBM)
    shape = jax.ShapeDtypeStruct
    params = pltpu.CompilerParams(vmem_limit_bytes=24 * MIB)
    edge = shape((EDGE, channels), BF16)
    to_pair, to_other = pl.pallas_call(
        edges_kernel,
        out_shape=[edge, edge],
        in_specs=[hbm] * 2,
        out_specs=[vmem] * 2,
        scratch_shapes=[pltpu.VMEM((TILE, channels), BF16)] * 2
        + [pltpu.SemaphoreType.DMA((2,))],
        compiler_params=params,
        name="edges",
    )(
        pltpu.with_memory_space_constraint(block, pltpu.HBM),
        pltpu.with_memory_space_constraint(conv_first, pltpu.HBM),
    )
    pair = lax.ppermute(to_pair, ("seq", "batch"), swaps(0))
    other = lax.ppermute(to_other, ("seq", "batch"), swaps(1))
    first = pl.pallas_call(
        functools.partial(first_kernel, count=lax.axis_size("seq")),
        out_shape=shape((circle, width), BF16),
        in_specs=[vmem] * 4,
        out_specs=vmem,
        scratch_shapes=[pltpu.VMEM((circle, channels), BF16), pltpu.VMEM((circle, width), F32)],
        compiler_params=params,
        name="first",
    )(block, pair, other, conv_first)
    half = heads // 2
    fixed = dict(heads=heads, head=head, spread=spread)
    unit = shape((rows, 3 * head), BF16)
    scale_scratch = [pltpu.SMEM(logit_scale.shape, F32), pltpu.SemaphoreType.DMA]
    hidden, *units = pl.pallas_call(
        functools.partial(second_kernel, **fixed),
        out_shape=[shape((rows, width), BF16)] + [unit] * half,
        in_specs=[vmem] * 3 + [hbm],
        out_specs=[vmem] * (1 + half),
        scratch_shapes=[pltpu.VMEM((circle, width), F32)] + scale_scratch,
        compiler_params=params,
        name="second",
    )(first, conv_second, qkv_weight, logit_scale)
    units += pl.pallas_call(
        functools.partial(third_kernel, **fixed),
        out_shape=[unit] * (heads - half),
        in_specs=[vmem] * 2 + [hbm],
        out_specs=[vmem] * (heads - half),
        scratch_shapes=scale_scratch,
        compiler_params=pltpu.CompilerParams(vmem_limit_bytes=24 * MIB),
        name="third",
    )(hidden, qkv_weight, logit_scale)
    return [hidden, *units]


def scores_of(queries, keys):
    return lax.dot_general(
        queries, keys, (((1,), (1,)), ((), ())), preferred_element_type=F32
    )


def attend_units(queries, units, wide_sums=False):
    head = queries.shape[1]
    scores = [scores_of(queries, unit[:, head : 2 * head]) for unit in units]
    top = functools.reduce(jnp.maximum, [jnp.max(s, axis=1, keepdims=True) for s in scores])
    weights = [jnp.exp(s - top) for s in scores]
    values = jnp.concatenate([unit[:, 2 * head :] for unit in units], axis=0)
    if wide_sums:
        values = jnp.concatenate([values, jnp.ones_like(values)], axis=1)
    else:
        total = functools.reduce(jnp.add, [jnp.sum(w, axis=1, keepdims=True) for w in weights])
    weights = jnp.concatenate([w.astype(BF16) for w in weights], axis=1)
    mixed = jnp.dot(weights, values, preferred_element_type=F32)
    return (top, mixed[:, head:], mixed[:, :head]) if wide_sums else (top, total, mixed)


def attend_all_kernel(*refs, head, count):
    units, outs = refs[:-count], refs[-count:]
    for i in range(count):
        _, total, mixed = attend_units(units[i][:, 0:head], units)
        outs[i][...] = (mixed / total).astype(BF16)


def attend_some_kernel(*refs, head, count):
    units, (tops, totals, sums) = refs[:-3], refs[-3:]
    rows = units[0].shape[0]
    for i in range(count):
        part = slice(i * rows, (i + 1) * rows)
        top, total, sums[part] = attend_units(units[i][:, 0:head], units)
        tops[part] = jnp.broadcast_to(top, (rows, head))
        totals[part] = jnp.broadcast_to(total, (rows, head))


def attend_rest_kernel(*refs, head, count):
    units, (tops, totals, sums), outs = refs[: -3 - count], refs[-3 - count : -count], refs[-count:]
    rows = units[0].shape[0]
    for i in range(count):
        part = slice(i * rows, (i + 1) * rows)
        top, total, mixed = attend_units(units[i][:, 0:head], units[count:], wide_sums=True)
        top = jnp.broadcast_to(top, (rows, head))
        new_top = jnp.maximum(top, tops[part])
        old, new = jnp.exp(tops[part] - new_top), jnp.exp(top - new_top)
        total = totals[part] * old + total * new
        outs[i][...] = ((sums[part] * old + mixed * new) / total).astype(BF16)


def attend(kernel, count, out_shape, operands, name):
    vmem = pl.BlockSpec(memory_space=pltpu.VMEM)
    head = operands[0].shape[1] // 3
    return pl.pallas_call(
        functools.partial(kernel, head=head, count=count),
        out_shape=out_shape,
        in_specs=[vmem] * len(operands),
        out_specs=[vmem] * len(out_shape),
        compiler_params=pltpu.CompilerParams(vmem_limit_bytes=24 * MIB),
        name=name,
    )(*operands)


def attention(own, swap):
    half = len(own) // 2
    rows, wide = own[0].shape
    shape = jax.ShapeDtypeStruct
    result = [shape((rows, wide // 3), BF16)] * half
    partial = [shape((half * rows, wide // 3), F32)] * 3
    far, near = own[:half], own[half:]
    other = [swap(unit) for unit in own]
    last = other[half - 1]
    most = [*far, *near, *other[: half - 1], *other[half:]]
    part = attend(attend_some_kernel, half, partial, most, "most")
    far_outs = attend(attend_rest_kernel, half, result, [*far, last, *part], "last")
    far_outs, near = lax.optimization_barrier((far_outs, near))
    near_outs = attend(attend_all_kernel, half, result, [*near, *far, *other], "near")
    return [*far_outs, *near_outs]


def finish_kernel(hidden_ref, weight_ref, *rest, spread):
    mixed, out_ref = rest[:-1], rest[-1]
    g = lax.axis_index("seq")
    head = mixed[0].shape[1]
    total = hidden_ref[...].astype(F32)
    for r in range(len(mixed)):
        h = head_of(r, g, len(mixed)) if spread else r
        at = pl.multiple_of(h * head, head)
        total += jnp.dot(
            mixed[r][...], weight_ref[pl.ds(at, head), :], preferred_element_type=F32
        )
    out_ref[...] = total.astype(out_ref.dtype)


def finish(hidden, out_weight, mixed, spread):
    vmem = pl.BlockSpec(memory_space=pltpu.VMEM)
    return pl.pallas_call(
        functools.partial(finish_kernel, spread=spread),
        out_shape=jax.ShapeDtypeStruct(hidden.shape, BF16),
        in_specs=[vmem] * (2 + len(mixed)),
        out_specs=vmem,
        compiler_params=pltpu.CompilerParams(vmem_limit_bytes=32 * MIB),
        name="finish",
    )(hidden, out_weight, *mixed)


def routes(seq_count, batch_count, heads):
    half = heads // 2
    rounds = []
    for r in range(heads):
        pairs = []
        for g in range(seq_count):
            for b in range(batch_count):
                h = head_of(r, g, heads)
                chip = heads * (h // half) + half * (b % 2) + h % half
                core = (g // half + r // half) % 2
                target = chip * batch_count + b - b % 2 + core
                pairs.append((g * batch_count + b, target))
        rounds.append(pairs)
    return rounds


def by_heads(sequence_input, conv_first, conv_second, qkv_weight, out_weight, logit_scale):
    heads = logit_scale.shape[0]
    count = lax.axis_size("seq")
    batch_count = lax.axis_size("batch")
    hidden, *units = stem(
        sequence_input, conv_first, conv_second, qkv_weight, logit_scale, True
    )
    both = ("seq", "batch")
    rounds = routes(count, batch_count, heads)
    own = [lax.ppermute(unit, both, pairs) for unit, pairs in zip(units, rounds)]
    cores = [(b, b ^ 1) for b in range(batch_count)]
    outs = attention(own, lambda unit: lax.ppermute(unit, "batch", cores))
    mixed = [
        lax.ppermute(out, both, [(target, source) for source, target in pairs])
        for out, pairs in zip(outs, rounds)
    ]
    return finish(hidden, out_weight, mixed, True)


def by_gather(sequence_input, conv_first, conv_second, qkv_weight, out_weight, logit_scale):
    heads = logit_scale.shape[0]
    count = lax.axis_size("seq")
    hidden, *units = stem(
        sequence_input, conv_first, conv_second, qkv_weight, logit_scale, False
    )
    head = units[0].shape[1] // 3
    pairs = jnp.concatenate([unit[:, head:] for unit in units], axis=1)
    everywhere = lax.all_gather(pairs, "seq", axis=0, tiled=True)
    mixed = []
    for h in range(heads):
        at = 2 * h * head
        scores = lax.dot_general(
            units[h][:, :head],
            everywhere[:, at : at + head],
            (((1,), (1,)), ((), ())),
            preferred_element_type=F32,
        )
        weights = jnp.exp(scores - jnp.max(scores, axis=1, keepdims=True))
        denominators = jnp.sum(weights, axis=1, keepdims=True)
        out = jnp.dot(
            weights.astype(BF16),
            everywhere[:, at + head : at + 2 * head],
            preferred_element_type=F32,
        )
        mixed.append((out / denominators).astype(BF16))
    return finish(hidden, out_weight, mixed, False)


def solution(mesh):
    def body(*args):
        heads = args[-1].shape[0]
        fits = heads == 4 and mesh.shape["seq"] == 2 * heads and mesh.shape["batch"] % 2 == 0
        return (by_heads if fits else by_gather)(*args)

    in_specs = (P(("batch", "seq"), None), P(), P(), P(), P(), P())
    out_specs = P(("batch", "seq"), None)
    return jax.shard_map(body, mesh=mesh, in_specs=in_specs, out_specs=out_specs, check_vma=False)
```

```python
import functools
import math

import jax
import jax.numpy as jnp
from jax import lax
from jax.experimental import pallas as pl
from jax.experimental.pallas import tpu as pltpu
from jax.sharding import PartitionSpec as P

F32 = jnp.float32
BF16 = jnp.bfloat16
EDGE = 8
TILE = 16
TAPS = 5
MIB = 1 << 20


def head_rms(tensor):
    return tensor * lax.rsqrt(jnp.mean(tensor * tensor, axis=-1, keepdims=True) + 1e-06)


def edges_kernel(x_hbm, w1_hbm, to_pair, to_other, first, last, sems):
    rows = x_hbm.shape[0]
    copies = [
        pltpu.make_async_copy(x_hbm.at[pl.ds(0, TILE)], first, sems.at[0]),
        pltpu.make_async_copy(x_hbm.at[pl.ds(rows - TILE, TILE)], last, sems.at[1]),
    ]
    for copy in copies:
        copy.start()
    for copy in copies:
        copy.wait()
    even = lax.axis_index("seq") % 2 == 0
    begin = first[...].astype(F32)[:EDGE]
    end = last[...].astype(F32)[TILE - EDGE :]
    to_pair[...] = jnp.where(even, end, begin).astype(BF16)
    to_other[...] = jnp.where(even, begin, end).astype(BF16)


def rolled(product, j):
    shift = (TAPS // 2 - j) % product.shape[0]
    return product if shift == 0 else pltpu.roll(product, shift, 0)


def first_kernel(x_ref, pair_ref, other_ref, w1, first_ref, x, total, *, count):
    rows = x_ref.shape[0]
    g = lax.axis_index("seq")
    even = g % 2 == 0
    has_before = (g > 0).astype(F32)
    has_after = (g < count - 1).astype(F32)
    pair, other = pair_ref[...].astype(F32), other_ref[...].astype(F32)
    after = jnp.where(even, pair, other) * has_after
    before = jnp.where(even, other, pair) * has_before
    x[0:rows] = x_ref[...]
    x[rows:] = jnp.concatenate([after, before], axis=0).astype(BF16)
    for j in range(TAPS):
        product = rolled(jnp.dot(x[...], w1[j], preferred_element_type=F32), j)
        if j == 0:
            total[...] = product
        else:
            total[...] += product
    first_ref[0:rows] = jax.nn.gelu(total[0:rows]).astype(BF16)
    after = jax.nn.gelu(total[rows : rows + EDGE]) * has_after
    before = jax.nn.gelu(total[rows + EDGE :]) * has_before
    first_ref[rows:] = jnp.concatenate([after, before], axis=0).astype(BF16)


def second_kernel(first_ref, w2, wqkv, scale_hbm, *rest, heads, head, spread):
    hidden_ref, units, (total, scale_ref, sem) = rest[0], rest[1:-3], rest[-3:]
    scale_copy = pltpu.make_async_copy(scale_hbm, scale_ref, sem)
    scale_copy.start()
    rows = hidden_ref.shape[0]
    for j in range(TAPS):
        product = rolled(jnp.dot(first_ref[...], w2[j], preferred_element_type=F32), j)
        if j == 0:
            total[...] = product
        else:
            total[...] += product
    hidden_ref[...] = (first_ref[0:rows].astype(F32) + total[0:rows]).astype(BF16)
    scale_copy.wait()
    g = lax.axis_index("seq")
    project(hidden_ref, wqkv, scale_ref, units, g, range(len(units)), heads, head, spread)


def project(hidden_ref, wqkv, scale_ref, units, g, rounds, heads, head, spread):
    width = heads * head
    hidden = hidden_ref[...]
    for unit, r in zip(units, rounds):
        h = head_of(r, g, heads) if spread else r
        at = pl.multiple_of(h * head, head)
        weight = jnp.concatenate(
            [wqkv[:, pl.ds(part * width + at, head)] for part in range(3)], axis=1
        )
        projected = jnp.dot(hidden, weight, preferred_element_type=F32)
        q = head_rms(projected[:, :head]) * (scale_ref[h] / math.sqrt(head))
        unit[:, 0:head] = q.astype(BF16)
        unit[:, head : 2 * head] = head_rms(projected[:, head : 2 * head]).astype(BF16)
        unit[:, 2 * head :] = projected[:, 2 * head :].astype(BF16)


def third_kernel(hidden_ref, wqkv, scale_hbm, *rest, heads, head, spread):
    units, (scale_ref, sem) = rest[:-2], rest[-2:]
    scale_copy = pltpu.make_async_copy(scale_hbm, scale_ref, sem)
    scale_copy.start()
    scale_copy.wait()
    g = lax.axis_index("seq")
    rounds = range(heads - len(units), heads)
    project(hidden_ref, wqkv, scale_ref, units, g, rounds, heads, head, spread)


def head_of(r, g, heads):
    half = heads // 2
    side = g // heads
    return half * (side ^ 1 ^ (r // half)) + ((r % half) ^ (g % half))


def swaps(offset):
    count, batch_count = lax.axis_size("seq"), lax.axis_size("batch")
    pairs = []
    for g in range(count):
        for b in range(batch_count):
            to = ((g + offset) ^ 1) - offset
            target = (to, b) if 0 <= to < count else (g, b ^ 1 if b ^ 1 < batch_count else b)
            pairs.append((g * batch_count + b, target[0] * batch_count + target[1]))
    return pairs


def stem(block, conv_first, conv_second, qkv_weight, logit_scale, spread):
    rows, channels = block.shape
    width = conv_first.shape[2]
    heads = logit_scale.shape[0]
    head = qkv_weight.shape[1] // 3 // heads
    circle = rows + 2 * EDGE
    vmem = pl.BlockSpec(memory_space=pltpu.VMEM)
    hbm = pl.BlockSpec(memory_space=pltpu.HBM)
    shape = jax.ShapeDtypeStruct
    params = pltpu.CompilerParams(vmem_limit_bytes=24 * MIB)
    edge = shape((EDGE, channels), BF16)
    to_pair, to_other = pl.pallas_call(
        edges_kernel,
        out_shape=[edge, edge],
        in_specs=[hbm] * 2,
        out_specs=[vmem] * 2,
        scratch_shapes=[pltpu.VMEM((TILE, channels), BF16)] * 2
        + [pltpu.SemaphoreType.DMA((2,))],
        compiler_params=params,
        name="edges",
    )(
        pltpu.with_memory_space_constraint(block, pltpu.HBM),
        pltpu.with_memory_space_constraint(conv_first, pltpu.HBM),
    )
    pair = lax.ppermute(to_pair, ("seq", "batch"), swaps(0))
    other = lax.ppermute(to_other, ("seq", "batch"), swaps(1))
    first = pl.pallas_call(
        functools.partial(first_kernel, count=lax.axis_size("seq")),
        out_shape=shape((circle, width), BF16),
        in_specs=[vmem] * 4,
        out_specs=vmem,
        scratch_shapes=[pltpu.VMEM((circle, channels), BF16), pltpu.VMEM((circle, width), F32)],
        compiler_params=params,
        name="first",
    )(block, pair, other, conv_first)
    half = 1
    fixed = dict(heads=heads, head=head, spread=spread)
    unit = shape((rows, 3 * head), BF16)
    scale_scratch = [pltpu.SMEM(logit_scale.shape, F32), pltpu.SemaphoreType.DMA]
    hidden, *units = pl.pallas_call(
        functools.partial(second_kernel, **fixed),
        out_shape=[shape((rows, width), BF16)] + [unit] * half,
        in_specs=[vmem] * 3 + [hbm],
        out_specs=[vmem] * (1 + half),
        scratch_shapes=[pltpu.VMEM((circle, width), F32)] + scale_scratch,
        compiler_params=params,
        name="second",
    )(first, conv_second, qkv_weight, logit_scale)
    units += pl.pallas_call(
        functools.partial(third_kernel, **fixed),
        out_shape=[unit] * (heads - half),
        in_specs=[vmem] * 2 + [hbm],
        out_specs=[vmem] * (heads - half),
        scratch_shapes=scale_scratch,
        compiler_params=pltpu.CompilerParams(vmem_limit_bytes=24 * MIB),
        name="third",
    )(hidden, qkv_weight, logit_scale)
    return [hidden, *units]


def scores_of(queries, keys):
    return lax.dot_general(
        queries, keys, (((1,), (1,)), ((), ())), preferred_element_type=F32
    )


def attend_units(queries, units, wide_sums=False):
    head = queries.shape[1]
    scores = [scores_of(queries, unit[:, head : 2 * head]) for unit in units]
    top = functools.reduce(jnp.maximum, [jnp.max(s, axis=1, keepdims=True) for s in scores])
    weights = [jnp.exp(s - top) for s in scores]
    values = jnp.concatenate([unit[:, 2 * head :] for unit in units], axis=0)
    if wide_sums:
        values = jnp.concatenate([values, jnp.ones_like(values)], axis=1)
    else:
        total = functools.reduce(jnp.add, [jnp.sum(w, axis=1, keepdims=True) for w in weights])
    weights = jnp.concatenate([w.astype(BF16) for w in weights], axis=1)
    mixed = jnp.dot(weights, values, preferred_element_type=F32)
    return (top, mixed[:, head:], mixed[:, :head]) if wide_sums else (top, total, mixed)


def attend_all_kernel(*refs, head, count):
    units, outs = refs[:-count], refs[-count:]
    for i in range(count):
        _, total, mixed = attend_units(units[i][:, 0:head], units)
        outs[i][...] = (mixed / total).astype(BF16)


def attend_some_kernel(*refs, head, count):
    units, (tops, totals, sums) = refs[:-3], refs[-3:]
    rows = units[0].shape[0]
    for i in range(count):
        part = slice(i * rows, (i + 1) * rows)
        top, total, sums[part] = attend_units(units[i][:, 0:head], units)
        tops[part] = jnp.broadcast_to(top, (rows, head))
        totals[part] = jnp.broadcast_to(total, (rows, head))


def attend_rest_kernel(*refs, head, count):
    units, (tops, totals, sums), outs = refs[: -3 - count], refs[-3 - count : -count], refs[-count:]
    rows = units[0].shape[0]
    for i in range(count):
        part = slice(i * rows, (i + 1) * rows)
        top, total, mixed = attend_units(units[i][:, 0:head], units[count:], wide_sums=True)
        top = jnp.broadcast_to(top, (rows, head))
        new_top = jnp.maximum(top, tops[part])
        old, new = jnp.exp(tops[part] - new_top), jnp.exp(top - new_top)
        total = totals[part] * old + total * new
        outs[i][...] = ((sums[part] * old + mixed * new) / total).astype(BF16)


def attend(kernel, count, out_shape, operands, name):
    vmem = pl.BlockSpec(memory_space=pltpu.VMEM)
    head = operands[0].shape[1] // 3
    return pl.pallas_call(
        functools.partial(kernel, head=head, count=count),
        out_shape=out_shape,
        in_specs=[vmem] * len(operands),
        out_specs=[vmem] * len(out_shape),
        compiler_params=pltpu.CompilerParams(vmem_limit_bytes=24 * MIB),
        name=name,
    )(*operands)


def attention(own, swap):
    rows, wide = own[0].shape
    shape = jax.ShapeDtypeStruct
    steps = [0, 1], [2, 3]
    result = [shape((rows, wide // 3), BF16)] * len(steps[0])
    partial = [shape((len(steps[0]) * rows, wide // 3), F32)] * 3
    other = [swap(unit) for unit in own]
    last = len(own) // 2 - 1
    queries = [own[r] for r in steps[0]]
    most = queries + [own[r] for r in steps[1]] + other[:last] + other[last + 1 :]
    part = attend(attend_some_kernel, len(queries), partial, most, "most")
    outs = attend(attend_rest_kernel, len(queries), result, [*queries, other[last], *part], "last")
    outs, own = lax.optimization_barrier((outs, own))
    queries = [own[r] for r in steps[1]]
    keys = queries + [own[r] for r in steps[0]] + other
    outs = outs + attend(attend_all_kernel, len(queries), result, keys, "near")
    return outs, steps[0] + steps[1]


def finish_kernel(hidden_ref, weight_ref, *rest, rounds, spread):
    mixed, out_ref = rest[:-1], rest[-1]
    g = lax.axis_index("seq")
    head = mixed[0].shape[1]
    total = hidden_ref[...].astype(F32)
    for r, part in zip(rounds, mixed):
        h = head_of(r, g, len(mixed)) if spread else r
        at = pl.multiple_of(h * head, head)
        total += jnp.dot(
            part[...], weight_ref[pl.ds(at, head), :], preferred_element_type=F32
        )
    out_ref[...] = total.astype(out_ref.dtype)


def finish(hidden, out_weight, mixed, rounds, spread):
    vmem = pl.BlockSpec(memory_space=pltpu.VMEM)
    return pl.pallas_call(
        functools.partial(finish_kernel, rounds=rounds, spread=spread),
        out_shape=jax.ShapeDtypeStruct(hidden.shape, BF16),
        in_specs=[vmem] * (2 + len(mixed)),
        out_specs=vmem,
        compiler_params=pltpu.CompilerParams(vmem_limit_bytes=32 * MIB),
        name="finish",
    )(hidden, out_weight, *mixed)


def routes(seq_count, batch_count, heads):
    half = heads // 2
    rounds = []
    for r in range(heads):
        pairs = []
        for g in range(seq_count):
            for b in range(batch_count):
                h = head_of(r, g, heads)
                chip = heads * (h // half) + half * (b % 2) + h % half
                core = (g // half + r // half) % 2
                target = chip * batch_count + b - b % 2 + core
                pairs.append((g * batch_count + b, target))
        rounds.append(pairs)
    return rounds


def by_heads(sequence_input, conv_first, conv_second, qkv_weight, out_weight, logit_scale):
    heads = logit_scale.shape[0]
    count = lax.axis_size("seq")
    batch_count = lax.axis_size("batch")
    hidden, *units = stem(
        sequence_input, conv_first, conv_second, qkv_weight, logit_scale, True
    )
    both = ("seq", "batch")
    rounds = routes(count, batch_count, heads)
    own = [lax.ppermute(unit, both, pairs) for unit, pairs in zip(units, rounds)]
    cores = [(b, b ^ 1) for b in range(batch_count)]
    outs, order = attention(own, lambda unit: lax.ppermute(unit, "batch", cores))
    mixed = [
        lax.ppermute(out, both, [(target, source) for source, target in rounds[r]])
        for out, r in zip(outs, order)
    ]
    return finish(hidden, out_weight, mixed, order, True)


def by_gather(sequence_input, conv_first, conv_second, qkv_weight, out_weight, logit_scale):
    heads = logit_scale.shape[0]
    count = lax.axis_size("seq")
    hidden, *units = stem(
        sequence_input, conv_first, conv_second, qkv_weight, logit_scale, False
    )
    head = units[0].shape[1] // 3
    pairs = jnp.concatenate([unit[:, head:] for unit in units], axis=1)
    everywhere = lax.all_gather(pairs, "seq", axis=0, tiled=True)
    mixed = []
    for h in range(heads):
        at = 2 * h * head
        scores = lax.dot_general(
            units[h][:, :head],
            everywhere[:, at : at + head],
            (((1,), (1,)), ((), ())),
            preferred_element_type=F32,
        )
        weights = jnp.exp(scores - jnp.max(scores, axis=1, keepdims=True))
        denominators = jnp.sum(weights, axis=1, keepdims=True)
        out = jnp.dot(
            weights.astype(BF16),
            everywhere[:, at + head : at + 2 * head],
            preferred_element_type=F32,
        )
        mixed.append((out / denominators).astype(BF16))
    return finish(hidden, out_weight, mixed, range(heads), False)


def solution(mesh):
    def body(*args):
        heads = args[-1].shape[0]
        fits = heads == 4 and mesh.shape["seq"] == 2 * heads and mesh.shape["batch"] % 2 == 0
        return (by_heads if fits else by_gather)(*args)

    in_specs = (P(("batch", "seq"), None), P(), P(), P(), P(), P())
    out_specs = P(("batch", "seq"), None)
    return jax.shard_map(body, mesh=mesh, in_specs=in_specs, out_specs=out_specs, check_vma=False)
```

```python
import functools
import math

import jax
import jax.numpy as jnp
from jax import lax
from jax.experimental import pallas as pl
from jax.experimental.pallas import tpu as pltpu
from jax.sharding import PartitionSpec as P

F32 = jnp.float32
BF16 = jnp.bfloat16
EDGE = 8
TILE = 16
TAPS = 5
MIB = 1 << 20


def head_rms(tensor):
    return tensor * lax.rsqrt(jnp.mean(tensor * tensor, axis=-1, keepdims=True) + 1e-06)


def edges_kernel(x_hbm, w1_hbm, to_pair, to_other, first, last, sems):
    rows = x_hbm.shape[0]
    copies = [
        pltpu.make_async_copy(x_hbm.at[pl.ds(0, TILE)], first, sems.at[0]),
        pltpu.make_async_copy(x_hbm.at[pl.ds(rows - TILE, TILE)], last, sems.at[1]),
    ]
    for copy in copies:
        copy.start()
    for copy in copies:
        copy.wait()
    even = lax.axis_index("seq") % 2 == 0
    begin = first[...].astype(F32)[:EDGE]
    end = last[...].astype(F32)[TILE - EDGE :]
    to_pair[...] = jnp.where(even, end, begin).astype(BF16)
    to_other[...] = jnp.where(even, begin, end).astype(BF16)


def rolled(product, j):
    shift = (TAPS // 2 - j) % product.shape[0]
    return product if shift == 0 else pltpu.roll(product, shift, 0)


def first_kernel(x_ref, other_ref, pair_ref, w1, first_ref, x, total, *, count):
    rows = x_ref.shape[0]
    g = lax.axis_index("seq")
    even = g % 2 == 0
    has_before = (g > 0).astype(F32)
    has_after = (g < count - 1).astype(F32)
    pair, other = pair_ref[...].astype(F32), other_ref[...].astype(F32)
    after = jnp.where(even, pair, other) * has_after
    before = jnp.where(even, other, pair) * has_before
    x[0:rows] = x_ref[...]
    x[rows:] = jnp.concatenate([after, before], axis=0).astype(BF16)
    for j in range(TAPS):
        product = rolled(jnp.dot(x[...], w1[j], preferred_element_type=F32), j)
        if j == 0:
            total[...] = product
        else:
            total[...] += product
    first_ref[0:rows] = jax.nn.gelu(total[0:rows]).astype(BF16)
    after = jax.nn.gelu(total[rows : rows + EDGE]) * has_after
    before = jax.nn.gelu(total[rows + EDGE :]) * has_before
    first_ref[rows:] = jnp.concatenate([after, before], axis=0).astype(BF16)


def second_kernel(first_ref, w2, wqkv, scale_hbm, *rest, heads, head, spread):
    hidden_ref, units, (total, scale_ref, sem) = rest[0], rest[1:-3], rest[-3:]
    scale_copy = pltpu.make_async_copy(scale_hbm, scale_ref, sem)
    scale_copy.start()
    rows = hidden_ref.shape[0]
    for j in range(TAPS):
        product = rolled(jnp.dot(first_ref[...], w2[j], preferred_element_type=F32), j)
        if j == 0:
            total[...] = product
        else:
            total[...] += product
    hidden_ref[...] = (first_ref[0:rows].astype(F32) + total[0:rows]).astype(BF16)
    scale_copy.wait()
    g = lax.axis_index("seq")
    project(hidden_ref, wqkv, scale_ref, units, g, range(len(units)), heads, head, spread)


def project(hidden_ref, wqkv, scale_ref, units, g, rounds, heads, head, spread):
    width = heads * head
    hidden = hidden_ref[...]
    for unit, r in zip(units, rounds):
        h = head_of(r, g, heads) if spread else r
        at = pl.multiple_of(h * head, head)
        weight = jnp.concatenate(
            [wqkv[:, pl.ds(part * width + at, head)] for part in range(3)], axis=1
        )
        projected = jnp.dot(hidden, weight, preferred_element_type=F32)
        q = head_rms(projected[:, :head]) * (scale_ref[h] / math.sqrt(head))
        unit[:, 0:head] = q.astype(BF16)
        unit[:, head : 2 * head] = head_rms(projected[:, head : 2 * head]).astype(BF16)
        unit[:, 2 * head :] = projected[:, 2 * head :].astype(BF16)


def third_kernel(hidden_ref, wqkv, scale_hbm, *rest, heads, head, spread):
    units, (scale_ref, sem) = rest[:-2], rest[-2:]
    scale_copy = pltpu.make_async_copy(scale_hbm, scale_ref, sem)
    scale_copy.start()
    scale_copy.wait()
    g = lax.axis_index("seq")
    rounds = range(heads - len(units), heads)
    project(hidden_ref, wqkv, scale_ref, units, g, rounds, heads, head, spread)


def head_of(r, g, heads):
    half = heads // 2
    side = g // heads
    return half * (side ^ 1 ^ (r // half)) + ((r % half) ^ (g % half))


def swaps(offset):
    count, batch_count = lax.axis_size("seq"), lax.axis_size("batch")
    pairs = []
    for g in range(count):
        for b in range(batch_count):
            to = ((g + offset) ^ 1) - offset
            target = (to, b) if 0 <= to < count else (g, b ^ 1 if b ^ 1 < batch_count else b)
            pairs.append((g * batch_count + b, target[0] * batch_count + target[1]))
    return pairs


def stem(block, conv_first, conv_second, qkv_weight, logit_scale, spread):
    rows, channels = block.shape
    width = conv_first.shape[2]
    heads = logit_scale.shape[0]
    head = qkv_weight.shape[1] // 3 // heads
    circle = rows + 2 * EDGE
    vmem = pl.BlockSpec(memory_space=pltpu.VMEM)
    hbm = pl.BlockSpec(memory_space=pltpu.HBM)
    shape = jax.ShapeDtypeStruct
    params = pltpu.CompilerParams(vmem_limit_bytes=24 * MIB)
    edge = shape((EDGE, channels), BF16)
    to_pair, to_other = pl.pallas_call(
        edges_kernel,
        out_shape=[edge, edge],
        in_specs=[hbm] * 2,
        out_specs=[vmem] * 2,
        scratch_shapes=[pltpu.VMEM((TILE, channels), BF16)] * 2
        + [pltpu.SemaphoreType.DMA((2,))],
        compiler_params=params,
        name="edges",
    )(
        pltpu.with_memory_space_constraint(block, pltpu.HBM),
        pltpu.with_memory_space_constraint(conv_first, pltpu.HBM),
    )
    other = lax.ppermute(to_other, ("seq", "batch"), swaps(1))
    pair = lax.ppermute(to_pair, ("seq", "batch"), swaps(0))
    first = pl.pallas_call(
        functools.partial(first_kernel, count=lax.axis_size("seq")),
        out_shape=shape((circle, width), BF16),
        in_specs=[vmem] * 4,
        out_specs=vmem,
        scratch_shapes=[pltpu.VMEM((circle, channels), BF16), pltpu.VMEM((circle, width), F32)],
        compiler_params=params,
        name="first",
    )(block, other, pair, conv_first)
    half = 1
    fixed = dict(heads=heads, head=head, spread=spread)
    unit = shape((rows, 3 * head), BF16)
    scale_scratch = [pltpu.SMEM(logit_scale.shape, F32), pltpu.SemaphoreType.DMA]
    hidden, *units = pl.pallas_call(
        functools.partial(second_kernel, **fixed),
        out_shape=[shape((rows, width), BF16)] + [unit] * half,
        in_specs=[vmem] * 3 + [hbm],
        out_specs=[vmem] * (1 + half),
        scratch_shapes=[pltpu.VMEM((circle, width), F32)] + scale_scratch,
        compiler_params=params,
        name="second",
    )(first, conv_second, qkv_weight, logit_scale)
    units += pl.pallas_call(
        functools.partial(third_kernel, **fixed),
        out_shape=[unit] * (heads - half),
        in_specs=[vmem] * 2 + [hbm],
        out_specs=[vmem] * (heads - half),
        scratch_shapes=scale_scratch,
        compiler_params=pltpu.CompilerParams(vmem_limit_bytes=24 * MIB),
        name="third",
    )(hidden, qkv_weight, logit_scale)
    return [hidden, *units]


def scores_of(queries, keys):
    return lax.dot_general(
        queries, keys, (((1,), (1,)), ((), ())), preferred_element_type=F32
    )


def attend_units(queries, units, wide_sums=False):
    head = queries.shape[1]
    scores = [scores_of(queries, unit[:, head : 2 * head]) for unit in units]
    top = functools.reduce(jnp.maximum, [jnp.max(s, axis=1, keepdims=True) for s in scores])
    weights = [jnp.exp(s - top) for s in scores]
    values = jnp.concatenate([unit[:, 2 * head :] for unit in units], axis=0)
    if wide_sums:
        values = jnp.concatenate([values, jnp.ones_like(values)], axis=1)
    else:
        total = functools.reduce(jnp.add, [jnp.sum(w, axis=1, keepdims=True) for w in weights])
    weights = jnp.concatenate([w.astype(BF16) for w in weights], axis=1)
    mixed = jnp.dot(weights, values, preferred_element_type=F32)
    return (top, mixed[:, head:], mixed[:, :head]) if wide_sums else (top, total, mixed)


def attend_all_kernel(*refs, head, count):
    units, outs = refs[:-count], refs[-count:]
    for i in range(count):
        _, total, mixed = attend_units(units[i][:, 0:head], units)
        outs[i][...] = (mixed / total).astype(BF16)


def attend_some_kernel(*refs, head, count):
    units, (tops, totals, sums) = refs[:-3], refs[-3:]
    rows = units[0].shape[0]
    for i in range(count):
        part = slice(i * rows, (i + 1) * rows)
        top, total, sums[part] = attend_units(units[i][:, 0:head], units)
        tops[part] = jnp.broadcast_to(top, (rows, head))
        totals[part] = jnp.broadcast_to(total, (rows, head))


def attend_rest_kernel(*refs, head, count):
    units, (tops, totals, sums), outs = refs[: -3 - count], refs[-3 - count : -count], refs[-count:]
    rows = units[0].shape[0]
    for i in range(count):
        part = slice(i * rows, (i + 1) * rows)
        top, total, mixed = attend_units(units[i][:, 0:head], units[count:], wide_sums=True)
        top = jnp.broadcast_to(top, (rows, head))
        new_top = jnp.maximum(top, tops[part])
        old, new = jnp.exp(tops[part] - new_top), jnp.exp(top - new_top)
        total = totals[part] * old + total * new
        outs[i][...] = ((sums[part] * old + mixed * new) / total).astype(BF16)


def attend(kernel, count, out_shape, operands, name):
    vmem = pl.BlockSpec(memory_space=pltpu.VMEM)
    head = operands[0].shape[1] // 3
    return pl.pallas_call(
        functools.partial(kernel, head=head, count=count),
        out_shape=out_shape,
        in_specs=[vmem] * len(operands),
        out_specs=[vmem] * len(out_shape),
        compiler_params=pltpu.CompilerParams(vmem_limit_bytes=24 * MIB),
        name=name,
    )(*operands)


def attention(own, swap):
    rows, wide = own[0].shape
    shape = jax.ShapeDtypeStruct
    steps = [0, 1], [2, 3]
    result = [shape((rows, wide // 3), BF16)] * len(steps[0])
    partial = [shape((len(steps[0]) * rows, wide // 3), F32)] * 3
    other = [swap(unit) for unit in own]
    last = len(own) // 2 - 1
    queries = [own[r] for r in steps[0]]
    most = queries + [own[r] for r in steps[1]] + other[:last] + other[last + 1 :]
    part = attend(attend_some_kernel, len(queries), partial, most, "most")
    outs = attend(attend_rest_kernel, len(queries), result, [*queries, other[last], *part], "last")
    outs, own = lax.optimization_barrier((outs, own))
    queries = [own[r] for r in steps[1]]
    keys = queries + [own[r] for r in steps[0]] + other
    outs = outs + attend(attend_all_kernel, len(queries), result, keys, "near")
    return outs, steps[0] + steps[1]


def finish_kernel(hidden_ref, weight_ref, *rest, rounds, spread):
    mixed, out_ref = rest[:-1], rest[-1]
    g = lax.axis_index("seq")
    head = mixed[0].shape[1]
    total = hidden_ref[...].astype(F32)
    for r, part in zip(rounds, mixed):
        h = head_of(r, g, len(mixed)) if spread else r
        at = pl.multiple_of(h * head, head)
        total += jnp.dot(
            part[...], weight_ref[pl.ds(at, head), :], preferred_element_type=F32
        )
    out_ref[...] = total.astype(out_ref.dtype)


def finish(hidden, out_weight, mixed, rounds, spread):
    vmem = pl.BlockSpec(memory_space=pltpu.VMEM)
    return pl.pallas_call(
        functools.partial(finish_kernel, rounds=rounds, spread=spread),
        out_shape=jax.ShapeDtypeStruct(hidden.shape, BF16),
        in_specs=[vmem] * (2 + len(mixed)),
        out_specs=vmem,
        compiler_params=pltpu.CompilerParams(vmem_limit_bytes=32 * MIB),
        name="finish",
    )(hidden, out_weight, *mixed)


def routes(seq_count, batch_count, heads):
    half = heads // 2
    rounds = []
    for r in range(heads):
        pairs = []
        for g in range(seq_count):
            for b in range(batch_count):
                h = head_of(r, g, heads)
                chip = heads * (h // half) + half * (b % 2) + h % half
                core = (g // half + r // half) % 2
                target = chip * batch_count + b - b % 2 + core
                pairs.append((g * batch_count + b, target))
        rounds.append(pairs)
    return rounds


def by_heads(sequence_input, conv_first, conv_second, qkv_weight, out_weight, logit_scale):
    heads = logit_scale.shape[0]
    count = lax.axis_size("seq")
    batch_count = lax.axis_size("batch")
    hidden, *units = stem(
        sequence_input, conv_first, conv_second, qkv_weight, logit_scale, True
    )
    both = ("seq", "batch")
    rounds = routes(count, batch_count, heads)
    own = [lax.ppermute(unit, both, pairs) for unit, pairs in zip(units, rounds)]
    cores = [(b, b ^ 1) for b in range(batch_count)]
    outs, order = attention(own, lambda unit: lax.ppermute(unit, "batch", cores))
    mixed = [
        lax.ppermute(out, both, [(target, source) for source, target in rounds[r]])
        for out, r in zip(outs, order)
    ]
    return finish(hidden, out_weight, mixed, order, True)


def by_gather(sequence_input, conv_first, conv_second, qkv_weight, out_weight, logit_scale):
    heads = logit_scale.shape[0]
    count = lax.axis_size("seq")
    hidden, *units = stem(
        sequence_input, conv_first, conv_second, qkv_weight, logit_scale, False
    )
    head = units[0].shape[1] // 3
    pairs = jnp.concatenate([unit[:, head:] for unit in units], axis=1)
    everywhere = lax.all_gather(pairs, "seq", axis=0, tiled=True)
    mixed = []
    for h in range(heads):
        at = 2 * h * head
        scores = lax.dot_general(
            units[h][:, :head],
            everywhere[:, at : at + head],
            (((1,), (1,)), ((), ())),
            preferred_element_type=F32,
        )
        weights = jnp.exp(scores - jnp.max(scores, axis=1, keepdims=True))
        denominators = jnp.sum(weights, axis=1, keepdims=True)
        out = jnp.dot(
            weights.astype(BF16),
            everywhere[:, at + head : at + 2 * head],
            preferred_element_type=F32,
        )
        mixed.append((out / denominators).astype(BF16))
    return finish(hidden, out_weight, mixed, range(heads), False)


def solution(mesh):
    def body(*args):
        heads = args[-1].shape[0]
        fits = heads == 4 and mesh.shape["seq"] == 2 * heads and mesh.shape["batch"] % 2 == 0
        return (by_heads if fits else by_gather)(*args)

    in_specs = (P(("batch", "seq"), None), P(), P(), P(), P(), P())
    out_specs = P(("batch", "seq"), None)
    return jax.shard_map(body, mesh=mesh, in_specs=in_specs, out_specs=out_specs, check_vma=False)
```

```python
import functools
import math

import jax
import jax.numpy as jnp
from jax import lax
from jax.experimental import pallas as pl
from jax.experimental.pallas import tpu as pltpu
from jax.sharding import PartitionSpec as P

F32 = jnp.float32
BF16 = jnp.bfloat16
EDGE = 8
REACH = 4
TILE = 16
TAPS = 5
MIB = 1 << 20


def head_rms(tensor):
    return tensor * lax.rsqrt(jnp.mean(tensor * tensor, axis=-1, keepdims=True) + 1e-06)


def edges_kernel(x_hbm, w1_hbm, to_pair, to_other, first, last, sems):
    rows = x_hbm.shape[0]
    copies = [
        pltpu.make_async_copy(x_hbm.at[pl.ds(0, TILE)], first, sems.at[0]),
        pltpu.make_async_copy(x_hbm.at[pl.ds(rows - TILE, TILE)], last, sems.at[1]),
    ]
    for copy in copies:
        copy.start()
    for copy in copies:
        copy.wait()
    even = lax.axis_index("seq") % 2 == 0
    begin = folded(first[...].astype(F32)[:REACH])
    end = folded(last[...].astype(F32)[TILE - REACH :])
    to_pair[...] = jnp.where(even, end, begin).astype(BF16)
    to_other[...] = jnp.where(even, begin, end).astype(BF16)


def folded(rows):
    half = rows.shape[1] // 2
    return jnp.concatenate([rows[:, :half], rows[:, half:]], axis=0)


def unfolded(rows):
    return jnp.concatenate([rows[:REACH], rows[REACH:]], axis=1)


def rolled(product, j):
    shift = (TAPS // 2 - j) % product.shape[0]
    return product if shift == 0 else pltpu.roll(product, shift, 0)


def first_kernel(x_ref, other_ref, pair_ref, w1, first_ref, x, total, *, count):
    rows = x_ref.shape[0]
    g = lax.axis_index("seq")
    even = g % 2 == 0
    has_before = (g > 0).astype(F32)
    has_after = (g < count - 1).astype(F32)
    pair, other = pair_ref[...].astype(F32), other_ref[...].astype(F32)
    rest = jnp.zeros((EDGE - REACH, x.shape[1]), F32)
    after = unfolded(jnp.where(even, pair, other)) * has_after
    before = unfolded(jnp.where(even, other, pair)) * has_before
    x[0:rows] = x_ref[...]
    x[rows:] = jnp.concatenate([after, rest, rest, before], axis=0).astype(BF16)
    for j in range(TAPS):
        product = rolled(jnp.dot(x[...], w1[j], preferred_element_type=F32), j)
        if j == 0:
            total[...] = product
        else:
            total[...] += product
    first_ref[0:rows] = jax.nn.gelu(total[0:rows]).astype(BF16)
    after = jax.nn.gelu(total[rows : rows + EDGE]) * has_after
    before = jax.nn.gelu(total[rows + EDGE :]) * has_before
    first_ref[rows:] = jnp.concatenate([after, before], axis=0).astype(BF16)


def second_kernel(first_ref, w2, wqkv, scale_hbm, *rest, heads, head, spread):
    hidden_ref, units, (total, scale_ref, sem) = rest[0], rest[1:-3], rest[-3:]
    scale_copy = pltpu.make_async_copy(scale_hbm, scale_ref, sem)
    scale_copy.start()
    rows = hidden_ref.shape[0]
    for j in range(TAPS):
        product = rolled(jnp.dot(first_ref[...], w2[j], preferred_element_type=F32), j)
        if j == 0:
            total[...] = product
        else:
            total[...] += product
    hidden_ref[...] = (first_ref[0:rows].astype(F32) + total[0:rows]).astype(BF16)
    scale_copy.wait()
    g = lax.axis_index("seq")
    project(hidden_ref, wqkv, scale_ref, units, g, range(len(units)), heads, head, spread)


def project(hidden_ref, wqkv, scale_ref, units, g, rounds, heads, head, spread):
    width = heads * head
    hidden = hidden_ref[...]
    for unit, r in zip(units, rounds):
        h = head_of(r, g, heads) if spread else r
        at = pl.multiple_of(h * head, head)
        weight = jnp.concatenate(
            [wqkv[:, pl.ds(part * width + at, head)] for part in range(3)], axis=1
        )
        projected = jnp.dot(hidden, weight, preferred_element_type=F32)
        q = head_rms(projected[:, :head]) * (scale_ref[h] / math.sqrt(head))
        unit[:, 0:head] = q.astype(BF16)
        unit[:, head : 2 * head] = head_rms(projected[:, head : 2 * head]).astype(BF16)
        unit[:, 2 * head :] = projected[:, 2 * head :].astype(BF16)


def third_kernel(hidden_ref, wqkv, scale_hbm, *rest, heads, head, spread):
    units, (scale_ref, sem) = rest[:-2], rest[-2:]
    scale_copy = pltpu.make_async_copy(scale_hbm, scale_ref, sem)
    scale_copy.start()
    scale_copy.wait()
    g = lax.axis_index("seq")
    rounds = range(heads - len(units), heads)
    project(hidden_ref, wqkv, scale_ref, units, g, rounds, heads, head, spread)


def head_of(r, g, heads):
    half = heads // 2
    side = g // heads
    return half * (side ^ 1 ^ (r // half)) + ((r % half) ^ (g % half))


def swaps(offset):
    count, batch_count = lax.axis_size("seq"), lax.axis_size("batch")
    pairs = []
    for g in range(count):
        for b in range(batch_count):
            to = ((g + offset) ^ 1) - offset
            target = (to, b) if 0 <= to < count else (g, b ^ 1 if b ^ 1 < batch_count else b)
            pairs.append((g * batch_count + b, target[0] * batch_count + target[1]))
    return pairs


def stem(block, conv_first, conv_second, qkv_weight, logit_scale, spread):
    rows, channels = block.shape
    width = conv_first.shape[2]
    heads = logit_scale.shape[0]
    head = qkv_weight.shape[1] // 3 // heads
    circle = rows + 2 * EDGE
    vmem = pl.BlockSpec(memory_space=pltpu.VMEM)
    hbm = pl.BlockSpec(memory_space=pltpu.HBM)
    shape = jax.ShapeDtypeStruct
    params = pltpu.CompilerParams(vmem_limit_bytes=24 * MIB)
    edge = shape((EDGE, channels // 2), BF16)
    to_pair, to_other = pl.pallas_call(
        edges_kernel,
        out_shape=[edge, edge],
        in_specs=[hbm] * 2,
        out_specs=[vmem] * 2,
        scratch_shapes=[pltpu.VMEM((TILE, channels), BF16)] * 2
        + [pltpu.SemaphoreType.DMA((2,))],
        compiler_params=params,
        name="edges",
    )(
        pltpu.with_memory_space_constraint(block, pltpu.HBM),
        pltpu.with_memory_space_constraint(conv_first, pltpu.HBM),
    )
    other = lax.ppermute(to_other, ("seq", "batch"), swaps(1))
    pair = lax.ppermute(to_pair, ("seq", "batch"), swaps(0))
    first = pl.pallas_call(
        functools.partial(first_kernel, count=lax.axis_size("seq")),
        out_shape=shape((circle, width), BF16),
        in_specs=[vmem] * 4,
        out_specs=vmem,
        scratch_shapes=[pltpu.VMEM((circle, channels), BF16), pltpu.VMEM((circle, width), F32)],
        compiler_params=params,
        name="first",
    )(block, other, pair, conv_first)
    half = 1
    fixed = dict(heads=heads, head=head, spread=spread)
    unit = shape((rows, 3 * head), BF16)
    scale_scratch = [pltpu.SMEM(logit_scale.shape, F32), pltpu.SemaphoreType.DMA]
    hidden, *units = pl.pallas_call(
        functools.partial(second_kernel, **fixed),
        out_shape=[shape((rows, width), BF16)] + [unit] * half,
        in_specs=[vmem] * 3 + [hbm],
        out_specs=[vmem] * (1 + half),
        scratch_shapes=[pltpu.VMEM((circle, width), F32)] + scale_scratch,
        compiler_params=params,
        name="second",
    )(first, conv_second, qkv_weight, logit_scale)
    units += pl.pallas_call(
        functools.partial(third_kernel, **fixed),
        out_shape=[unit] * (heads - half),
        in_specs=[vmem] * 2 + [hbm],
        out_specs=[vmem] * (heads - half),
        scratch_shapes=scale_scratch,
        compiler_params=pltpu.CompilerParams(vmem_limit_bytes=24 * MIB),
        name="third",
    )(hidden, qkv_weight, logit_scale)
    return [hidden, *units]


def scores_of(queries, keys):
    return lax.dot_general(
        queries, keys, (((1,), (1,)), ((), ())), preferred_element_type=F32
    )


def attend_units(queries, units, wide_sums=False):
    head = queries.shape[1]
    scores = [scores_of(queries, unit[:, head : 2 * head]) for unit in units]
    top = functools.reduce(jnp.maximum, [jnp.max(s, axis=1, keepdims=True) for s in scores])
    weights = [jnp.exp(s - top) for s in scores]
    values = jnp.concatenate([unit[:, 2 * head :] for unit in units], axis=0)
    if wide_sums:
        values = jnp.concatenate([values, jnp.ones_like(values)], axis=1)
    else:
        total = functools.reduce(jnp.add, [jnp.sum(w, axis=1, keepdims=True) for w in weights])
    weights = jnp.concatenate([w.astype(BF16) for w in weights], axis=1)
    mixed = jnp.dot(weights, values, preferred_element_type=F32)
    return (top, mixed[:, head:], mixed[:, :head]) if wide_sums else (top, total, mixed)


def attend_all_kernel(*refs, head, count):
    units, outs = refs[:-count], refs[-count:]
    for i in range(count):
        _, total, mixed = attend_units(units[i][:, 0:head], units)
        outs[i][...] = (mixed / total).astype(BF16)


def attend_some_kernel(*refs, head, count):
    units, (tops, totals, sums) = refs[:-3], refs[-3:]
    rows = units[0].shape[0]
    for i in range(count):
        part = slice(i * rows, (i + 1) * rows)
        top, total, sums[part] = attend_units(units[i][:, 0:head], units)
        tops[part] = jnp.broadcast_to(top, (rows, head))
        totals[part] = jnp.broadcast_to(total, (rows, head))


def attend_rest_kernel(*refs, head, count):
    units, (tops, totals, sums), outs = refs[: -3 - count], refs[-3 - count : -count], refs[-count:]
    rows = units[0].shape[0]
    for i in range(count):
        part = slice(i * rows, (i + 1) * rows)
        top, total, mixed = attend_units(units[i][:, 0:head], units[count:], wide_sums=True)
        top = jnp.broadcast_to(top, (rows, head))
        new_top = jnp.maximum(top, tops[part])
        old, new = jnp.exp(tops[part] - new_top), jnp.exp(top - new_top)
        total = totals[part] * old + total * new
        outs[i][...] = ((sums[part] * old + mixed * new) / total).astype(BF16)


def attend(kernel, count, out_shape, operands, name):
    vmem = pl.BlockSpec(memory_space=pltpu.VMEM)
    head = operands[0].shape[1] // 3
    return pl.pallas_call(
        functools.partial(kernel, head=head, count=count),
        out_shape=out_shape,
        in_specs=[vmem] * len(operands),
        out_specs=[vmem] * len(out_shape),
        compiler_params=pltpu.CompilerParams(vmem_limit_bytes=24 * MIB),
        name=name,
    )(*operands)


def attention(own, swap):
    rows, wide = own[0].shape
    shape = jax.ShapeDtypeStruct
    steps = [0, 1], [2, 3]
    result = [shape((rows, wide // 3), BF16)] * len(steps[0])
    partial = [shape((len(steps[0]) * rows, wide // 3), F32)] * 3
    other = [swap(unit) for unit in own]
    last = len(own) // 2 - 1
    queries = [own[r] for r in steps[0]]
    most = queries + [own[r] for r in steps[1]] + other[:last] + other[last + 1 :]
    part = attend(attend_some_kernel, len(queries), partial, most, "most")
    outs = attend(attend_rest_kernel, len(queries), result, [*queries, other[last], *part], "last")
    outs, own = lax.optimization_barrier((outs, own))
    queries = [own[r] for r in steps[1]]
    keys = queries + [own[r] for r in steps[0]] + other
    outs = outs + attend(attend_all_kernel, len(queries), result, keys, "near")
    return outs, steps[0] + steps[1]


def finish_kernel(hidden_ref, weight_ref, *rest, rounds, spread):
    mixed, out_ref = rest[:-1], rest[-1]
    g = lax.axis_index("seq")
    head = mixed[0].shape[1]
    heads = [head_of(r, g, len(mixed)) if spread else r for r in rounds]
    rows = [weight_ref[pl.ds(pl.multiple_of(h * head, head), head), :] for h in heads]
    attended = jnp.concatenate([part[...] for part in mixed], axis=1)
    projected = jnp.dot(attended, jnp.concatenate(rows, axis=0), preferred_element_type=F32)
    out_ref[...] = (hidden_ref[...].astype(F32) + projected).astype(out_ref.dtype)


def finish(hidden, out_weight, mixed, rounds, spread):
    vmem = pl.BlockSpec(memory_space=pltpu.VMEM)
    return pl.pallas_call(
        functools.partial(finish_kernel, rounds=rounds, spread=spread),
        out_shape=jax.ShapeDtypeStruct(hidden.shape, BF16),
        in_specs=[vmem] * (2 + len(mixed)),
        out_specs=vmem,
        compiler_params=pltpu.CompilerParams(vmem_limit_bytes=32 * MIB),
        name="finish",
    )(hidden, out_weight, *mixed)


def routes(seq_count, batch_count, heads):
    half = heads // 2
    rounds = []
    for r in range(heads):
        pairs = []
        for g in range(seq_count):
            for b in range(batch_count):
                h = head_of(r, g, heads)
                chip = heads * (h // half) + half * (b % 2) + h % half
                core = (g // half + r // half) % 2
                target = chip * batch_count + b - b % 2 + core
                pairs.append((g * batch_count + b, target))
        rounds.append(pairs)
    return rounds


def by_heads(sequence_input, conv_first, conv_second, qkv_weight, out_weight, logit_scale):
    heads = logit_scale.shape[0]
    count = lax.axis_size("seq")
    batch_count = lax.axis_size("batch")
    hidden, *units = stem(
        sequence_input, conv_first, conv_second, qkv_weight, logit_scale, True
    )
    both = ("seq", "batch")
    rounds = routes(count, batch_count, heads)
    own = [lax.ppermute(unit, both, pairs) for unit, pairs in zip(units, rounds)]
    cores = [(b, b ^ 1) for b in range(batch_count)]
    outs, order = attention(own, lambda unit: lax.ppermute(unit, "batch", cores))
    mixed = [
        lax.ppermute(out, both, [(target, source) for source, target in rounds[r]])
        for out, r in zip(outs, order)
    ]
    return finish(hidden, out_weight, mixed, order, True)


def by_gather(sequence_input, conv_first, conv_second, qkv_weight, out_weight, logit_scale):
    heads = logit_scale.shape[0]
    count = lax.axis_size("seq")
    hidden, *units = stem(
        sequence_input, conv_first, conv_second, qkv_weight, logit_scale, False
    )
    head = units[0].shape[1] // 3
    pairs = jnp.concatenate([unit[:, head:] for unit in units], axis=1)
    everywhere = lax.all_gather(pairs, "seq", axis=0, tiled=True)
    mixed = []
    for h in range(heads):
        at = 2 * h * head
        scores = lax.dot_general(
            units[h][:, :head],
            everywhere[:, at : at + head],
            (((1,), (1,)), ((), ())),
            preferred_element_type=F32,
        )
        weights = jnp.exp(scores - jnp.max(scores, axis=1, keepdims=True))
        denominators = jnp.sum(weights, axis=1, keepdims=True)
        out = jnp.dot(
            weights.astype(BF16),
            everywhere[:, at + head : at + 2 * head],
            preferred_element_type=F32,
        )
        mixed.append((out / denominators).astype(BF16))
    return finish(hidden, out_weight, mixed, range(heads), False)


def solution(mesh):
    def body(*args):
        heads = args[-1].shape[0]
        fits = heads == 4 and mesh.shape["seq"] == 2 * heads and mesh.shape["batch"] % 2 == 0
        return (by_heads if fits else by_gather)(*args)

    in_specs = (P(("batch", "seq"), None), P(), P(), P(), P(), P())
    out_specs = P(("batch", "seq"), None)
    return jax.shard_map(body, mesh=mesh, in_specs=in_specs, out_specs=out_specs, check_vma=False)
```

```python
import functools
import math

import jax
import jax.numpy as jnp
from jax import lax
from jax.experimental import pallas as pl
from jax.experimental.pallas import tpu as pltpu
from jax.sharding import PartitionSpec as P

F32 = jnp.float32
BF16 = jnp.bfloat16
EDGE = 8
REACH = 4
TILE = 16
TAPS = 5
MIB = 1 << 20


def head_rms(tensor):
    return tensor * lax.rsqrt(jnp.mean(tensor * tensor, axis=-1, keepdims=True) + 1e-06)


def edges_kernel(x_hbm, w1_hbm, to_pair, to_other, first, last, sems):
    rows = x_hbm.shape[0]
    copies = [
        pltpu.make_async_copy(x_hbm.at[pl.ds(0, TILE)], first, sems.at[0]),
        pltpu.make_async_copy(x_hbm.at[pl.ds(rows - TILE, TILE)], last, sems.at[1]),
    ]
    for copy in copies:
        copy.start()
    for copy in copies:
        copy.wait()
    even = lax.axis_index("seq") % 2 == 0
    begin = folded(first[...].astype(F32)[:REACH])
    end = folded(last[...].astype(F32)[TILE - REACH :])
    to_pair[...] = jnp.where(even, end, begin).astype(BF16)
    to_other[...] = jnp.where(even, begin, end).astype(BF16)


def folded(rows):
    half = rows.shape[1] // 2
    return jnp.concatenate([rows[:, :half], rows[:, half:]], axis=0)


def unfolded(rows):
    return jnp.concatenate([rows[:REACH], rows[REACH:]], axis=1)


def rolled(product, j):
    shift = (TAPS // 2 - j) % product.shape[0]
    return product if shift == 0 else pltpu.roll(product, shift, 0)


def first_kernel(x_ref, other_ref, pair_ref, w1, first_ref, x, total, *, count):
    rows = x_ref.shape[0]
    g = lax.axis_index("seq")
    even = g % 2 == 0
    has_before = (g > 0).astype(F32)
    has_after = (g < count - 1).astype(F32)
    pair, other = pair_ref[...].astype(F32), other_ref[...].astype(F32)
    rest = jnp.zeros((EDGE - REACH, x.shape[1]), F32)
    after = unfolded(jnp.where(even, pair, other)) * has_after
    before = unfolded(jnp.where(even, other, pair)) * has_before
    x[0:rows] = x_ref[...]
    x[rows:] = jnp.concatenate([after, rest, rest, before], axis=0).astype(BF16)
    for j in range(TAPS):
        product = rolled(jnp.dot(x[...], w1[j], preferred_element_type=F32), j)
        if j == 0:
            total[...] = product
        else:
            total[...] += product
    first_ref[0:rows] = jax.nn.gelu(total[0:rows]).astype(BF16)
    after = jax.nn.gelu(total[rows : rows + EDGE]) * has_after
    before = jax.nn.gelu(total[rows + EDGE :]) * has_before
    first_ref[rows:] = jnp.concatenate([after, before], axis=0).astype(BF16)


def second_kernel(first_ref, w2, wqkv, scale_hbm, *rest, heads, head, spread):
    hidden_ref, units, (total, scale_ref, sem) = rest[0], rest[1:-3], rest[-3:]
    scale_copy = pltpu.make_async_copy(scale_hbm, scale_ref, sem)
    scale_copy.start()
    rows = hidden_ref.shape[0]
    for j in range(TAPS):
        product = rolled(jnp.dot(first_ref[...], w2[j], preferred_element_type=F32), j)
        if j == 0:
            total[...] = product
        else:
            total[...] += product
    hidden_ref[...] = (first_ref[0:rows].astype(F32) + total[0:rows]).astype(BF16)
    scale_copy.wait()
    g = lax.axis_index("seq")
    project(hidden_ref, wqkv, scale_ref, units, g, range(len(units)), heads, head, spread)


def project(hidden_ref, wqkv, scale_ref, units, g, rounds, heads, head, spread):
    width = heads * head
    hidden = hidden_ref[...]
    for unit, r in zip(units, rounds):
        h = head_of(r, g, heads) if spread else r
        at = pl.multiple_of(h * head, head)
        weight = jnp.concatenate(
            [wqkv[:, pl.ds(part * width + at, head)] for part in range(3)], axis=1
        )
        projected = jnp.dot(hidden, weight, preferred_element_type=F32)
        q = head_rms(projected[:, :head]) * (scale_ref[h] / math.sqrt(head))
        unit[:, 0:head] = q.astype(BF16)
        unit[:, head : 2 * head] = head_rms(projected[:, head : 2 * head]).astype(BF16)
        unit[:, 2 * head :] = projected[:, 2 * head :].astype(BF16)


def third_kernel(hidden_ref, wqkv, scale_hbm, *rest, heads, head, spread):
    units, (scale_ref, sem) = rest[:-2], rest[-2:]
    scale_copy = pltpu.make_async_copy(scale_hbm, scale_ref, sem)
    scale_copy.start()
    scale_copy.wait()
    g = lax.axis_index("seq")
    rounds = range(heads - len(units), heads)
    project(hidden_ref, wqkv, scale_ref, units, g, rounds, heads, head, spread)


def head_of(r, g, heads):
    half = heads // 2
    side = g // heads
    return half * (side ^ 1 ^ (r // half)) + ((r % half) ^ (g % half))


def swaps(offset):
    count, batch_count = lax.axis_size("seq"), lax.axis_size("batch")
    pairs = []
    for g in range(count):
        for b in range(batch_count):
            to = ((g + offset) ^ 1) - offset
            target = (to, b) if 0 <= to < count else (g, b ^ 1 if b ^ 1 < batch_count else b)
            pairs.append((g * batch_count + b, target[0] * batch_count + target[1]))
    return pairs


def stem(block, conv_first, conv_second, qkv_weight, logit_scale, spread):
    rows, channels = block.shape
    width = conv_first.shape[2]
    heads = logit_scale.shape[0]
    head = qkv_weight.shape[1] // 3 // heads
    circle = rows + 2 * EDGE
    vmem = pl.BlockSpec(memory_space=pltpu.VMEM)
    hbm = pl.BlockSpec(memory_space=pltpu.HBM)
    shape = jax.ShapeDtypeStruct
    params = pltpu.CompilerParams(vmem_limit_bytes=24 * MIB)
    edge = shape((EDGE, channels // 2), BF16)
    to_pair, to_other = pl.pallas_call(
        edges_kernel,
        out_shape=[edge, edge],
        in_specs=[hbm] * 2,
        out_specs=[vmem] * 2,
        scratch_shapes=[pltpu.VMEM((TILE, channels), BF16)] * 2
        + [pltpu.SemaphoreType.DMA((2,))],
        compiler_params=params,
        name="edges",
    )(
        pltpu.with_memory_space_constraint(block, pltpu.HBM),
        pltpu.with_memory_space_constraint(conv_first, pltpu.HBM),
    )
    other = lax.ppermute(to_other, ("seq", "batch"), swaps(1))
    pair = lax.ppermute(to_pair, ("seq", "batch"), swaps(0))
    first = pl.pallas_call(
        functools.partial(first_kernel, count=lax.axis_size("seq")),
        out_shape=shape((circle, width), BF16),
        in_specs=[vmem] * 4,
        out_specs=vmem,
        scratch_shapes=[pltpu.VMEM((circle, channels), BF16), pltpu.VMEM((circle, width), F32)],
        compiler_params=params,
        name="first",
    )(block, other, pair, conv_first)
    half = 1
    fixed = dict(heads=heads, head=head, spread=spread)
    unit = shape((rows, 3 * head), BF16)
    scale_scratch = [pltpu.SMEM(logit_scale.shape, F32), pltpu.SemaphoreType.DMA]
    hidden, *units = pl.pallas_call(
        functools.partial(second_kernel, **fixed),
        out_shape=[shape((rows, width), BF16)] + [unit] * half,
        in_specs=[vmem] * 3 + [hbm],
        out_specs=[vmem] * (1 + half),
        scratch_shapes=[pltpu.VMEM((circle, width), F32)] + scale_scratch,
        compiler_params=params,
        name="second",
    )(first, conv_second, qkv_weight, logit_scale)
    units += pl.pallas_call(
        functools.partial(third_kernel, **fixed),
        out_shape=[unit] * (heads - half),
        in_specs=[vmem] * 2 + [hbm],
        out_specs=[vmem] * (heads - half),
        scratch_shapes=scale_scratch,
        compiler_params=pltpu.CompilerParams(vmem_limit_bytes=24 * MIB),
        name="third",
    )(hidden, qkv_weight, logit_scale)
    return [hidden, *units]


def scores_of(queries, keys):
    return lax.dot_general(
        queries, keys, (((1,), (1,)), ((), ())), preferred_element_type=F32
    )


def attend_units(queries, units, wide_sums=False):
    head = queries.shape[1]
    scores = [scores_of(queries, unit[:, head : 2 * head]) for unit in units]
    top = functools.reduce(jnp.maximum, [jnp.max(s, axis=1, keepdims=True) for s in scores])
    weights = [jnp.exp(s - top) for s in scores]
    values = jnp.concatenate([unit[:, 2 * head :] for unit in units], axis=0)
    if wide_sums:
        values = jnp.concatenate([values, jnp.ones_like(values)], axis=1)
    else:
        total = functools.reduce(jnp.add, [jnp.sum(w, axis=1, keepdims=True) for w in weights])
    weights = jnp.concatenate([w.astype(BF16) for w in weights], axis=1)
    mixed = jnp.dot(weights, values, preferred_element_type=F32)
    return (top, mixed[:, head:], mixed[:, :head]) if wide_sums else (top, total, mixed)


def attend_all_kernel(*refs, head, count):
    units, outs = refs[:-count], refs[-count:]
    for i in range(count):
        _, total, mixed = attend_units(units[i][:, 0:head], units)
        outs[i][...] = (mixed / total).astype(BF16)


def attend_some_kernel(*refs, head, count):
    units, (tops, totals, sums) = refs[:-3], refs[-3:]
    rows = units[0].shape[0]
    for i in range(count):
        part = slice(i * rows, (i + 1) * rows)
        top, total, sums[part] = attend_units(units[i][:, 0:head], units)
        tops[part] = jnp.broadcast_to(top, (rows, head))
        totals[part] = jnp.broadcast_to(total, (rows, head))


def attend_rest_kernel(*refs, head, count):
    units, (tops, totals, sums), outs = refs[: -3 - count], refs[-3 - count : -count], refs[-count:]
    rows = units[0].shape[0]
    for i in range(count):
        part = slice(i * rows, (i + 1) * rows)
        top, total, mixed = attend_units(units[i][:, 0:head], units[count:], wide_sums=True)
        top = jnp.broadcast_to(top, (rows, head))
        new_top = jnp.maximum(top, tops[part])
        old, new = jnp.exp(tops[part] - new_top), jnp.exp(top - new_top)
        total = totals[part] * old + total * new
        outs[i][...] = ((sums[part] * old + mixed * new) / total).astype(BF16)


def attend(kernel, count, out_shape, operands, name):
    vmem = pl.BlockSpec(memory_space=pltpu.VMEM)
    head = operands[0].shape[1] // 3
    return pl.pallas_call(
        functools.partial(kernel, head=head, count=count),
        out_shape=out_shape,
        in_specs=[vmem] * len(operands),
        out_specs=[vmem] * len(out_shape),
        compiler_params=pltpu.CompilerParams(vmem_limit_bytes=24 * MIB),
        name=name,
    )(*operands)


def attention(own, swap):
    rows, wide = own[0].shape
    shape = jax.ShapeDtypeStruct
    steps = [0, 1], [2, 3]
    result = [shape((rows, wide // 3), BF16)] * len(steps[0])
    partial = [shape((len(steps[0]) * rows, wide // 3), F32)] * 3
    other = [swap(unit) for unit in own]
    last = len(own) // 2 - 1
    queries = [own[r] for r in steps[0]]
    most = queries + [own[r] for r in steps[1]] + other[:last] + other[last + 1 :]
    part = attend(attend_some_kernel, len(queries), partial, most, "most")
    outs = attend(attend_rest_kernel, len(queries), result, [*queries, other[last], *part], "last")
    outs, own = lax.optimization_barrier((outs, own))
    queries = [own[r] for r in steps[1]]
    keys = queries + [own[r] for r in steps[0]] + other
    outs = outs + attend(attend_all_kernel, len(queries), result, keys, "near")
    return outs, steps[0] + steps[1]


def finish_kernel(hidden_ref, weight_ref, *rest, rounds, spread):
    mixed, out_ref = rest[:-1], rest[-1]
    g = lax.axis_index("seq")
    head = mixed[0].shape[1]
    heads = [head_of(r, g, len(mixed)) if spread else r for r in rounds]
    rows = [weight_ref[pl.ds(pl.multiple_of(h * head, head), head), :] for h in heads]
    attended = jnp.concatenate([part[...] for part in mixed], axis=1)
    projected = jnp.dot(attended, jnp.concatenate(rows, axis=0), preferred_element_type=F32)
    out_ref[...] = (hidden_ref[...].astype(F32) + projected).astype(out_ref.dtype)


def finish(hidden, out_weight, mixed, rounds, spread):
    vmem = pl.BlockSpec(memory_space=pltpu.VMEM)
    return pl.pallas_call(
        functools.partial(finish_kernel, rounds=rounds, spread=spread),
        out_shape=jax.ShapeDtypeStruct(hidden.shape, BF16),
        in_specs=[vmem] * (2 + len(mixed)),
        out_specs=vmem,
        compiler_params=pltpu.CompilerParams(vmem_limit_bytes=32 * MIB),
        name="finish",
    )(hidden, out_weight, *mixed)


def routes(seq_count, batch_count, heads):
    half = heads // 2
    rounds = []
    for r in range(heads):
        pairs = []
        for g in range(seq_count):
            for b in range(batch_count):
                h = head_of(r, g, heads)
                chip = heads * (h // half) + half * (b % 2) + h % half
                far = h // half != g // heads
                core = (g // half + (h // half if far else 1)) % 2
                target = chip * batch_count + b - b % 2 + core
                pairs.append((g * batch_count + b, target))
        rounds.append(pairs)
    return rounds


def by_heads(sequence_input, conv_first, conv_second, qkv_weight, out_weight, logit_scale):
    heads = logit_scale.shape[0]
    count = lax.axis_size("seq")
    batch_count = lax.axis_size("batch")
    hidden, *units = stem(
        sequence_input, conv_first, conv_second, qkv_weight, logit_scale, True
    )
    both = ("seq", "batch")
    rounds = routes(count, batch_count, heads)
    own = [lax.ppermute(unit, both, pairs) for unit, pairs in zip(units, rounds)]
    cores = [(b, b ^ 1) for b in range(batch_count)]
    outs, order = attention(own, lambda unit: lax.ppermute(unit, "batch", cores))
    mixed = [
        lax.ppermute(out, both, [(target, source) for source, target in rounds[r]])
        for out, r in zip(outs, order)
    ]
    return finish(hidden, out_weight, mixed, order, True)


def by_gather(sequence_input, conv_first, conv_second, qkv_weight, out_weight, logit_scale):
    heads = logit_scale.shape[0]
    count = lax.axis_size("seq")
    hidden, *units = stem(
        sequence_input, conv_first, conv_second, qkv_weight, logit_scale, False
    )
    head = units[0].shape[1] // 3
    pairs = jnp.concatenate([unit[:, head:] for unit in units], axis=1)
    everywhere = lax.all_gather(pairs, "seq", axis=0, tiled=True)
    mixed = []
    for h in range(heads):
        at = 2 * h * head
        scores = lax.dot_general(
            units[h][:, :head],
            everywhere[:, at : at + head],
            (((1,), (1,)), ((), ())),
            preferred_element_type=F32,
        )
        weights = jnp.exp(scores - jnp.max(scores, axis=1, keepdims=True))
        denominators = jnp.sum(weights, axis=1, keepdims=True)
        out = jnp.dot(
            weights.astype(BF16),
            everywhere[:, at + head : at + 2 * head],
            preferred_element_type=F32,
        )
        mixed.append((out / denominators).astype(BF16))
    return finish(hidden, out_weight, mixed, range(heads), False)


def solution(mesh):
    def body(*args):
        heads = args[-1].shape[0]
        fits = heads == 4 and mesh.shape["seq"] == 2 * heads and mesh.shape["batch"] % 2 == 0
        return (by_heads if fits else by_gather)(*args)

    in_specs = (P(("batch", "seq"), None), P(), P(), P(), P(), P())
    out_specs = P(("batch", "seq"), None)
    return jax.shard_map(body, mesh=mesh, in_specs=in_specs, out_specs=out_specs, check_vma=False)
```

```python
import functools
import math

import jax
import jax.numpy as jnp
from jax import lax
from jax.experimental import pallas as pl
from jax.experimental.pallas import tpu as pltpu
from jax.sharding import PartitionSpec as P

F32 = jnp.float32
BF16 = jnp.bfloat16
EDGE = 8
REACH = 4
TILE = 16
TAPS = 5
MIB = 1 << 20


def head_rms(tensor):
    return tensor * lax.rsqrt(jnp.mean(tensor * tensor, axis=-1, keepdims=True) + 1e-06)


def edges_kernel(x_hbm, w1_hbm, to_pair, to_other, first, last, sems):
    rows = x_hbm.shape[0]
    copies = [
        pltpu.make_async_copy(x_hbm.at[pl.ds(0, TILE)], first, sems.at[0]),
        pltpu.make_async_copy(x_hbm.at[pl.ds(rows - TILE, TILE)], last, sems.at[1]),
    ]
    for copy in copies:
        copy.start()
    for copy in copies:
        copy.wait()
    even = lax.axis_index("seq") % 2 == 0
    begin = folded(first[...].astype(F32)[:REACH])
    end = folded(last[...].astype(F32)[TILE - REACH :])
    to_pair[...] = jnp.where(even, end, begin).astype(BF16)
    to_other[...] = jnp.where(even, begin, end).astype(BF16)


def folded(rows):
    half = rows.shape[1] // 2
    return jnp.concatenate([rows[:, :half], rows[:, half:]], axis=0)


def unfolded(rows):
    return jnp.concatenate([rows[:REACH], rows[REACH:]], axis=1)


def rolled(product, j):
    shift = (TAPS // 2 - j) % product.shape[0]
    return product if shift == 0 else pltpu.roll(product, shift, 0)


def first_kernel(x_ref, other_ref, pair_ref, w1, first_ref, x, total, *, count):
    rows = x_ref.shape[0]
    g = lax.axis_index("seq")
    even = g % 2 == 0
    has_before = (g > 0).astype(F32)
    has_after = (g < count - 1).astype(F32)
    pair, other = pair_ref[...].astype(F32), other_ref[...].astype(F32)
    rest = jnp.zeros((EDGE - REACH, x.shape[1]), F32)
    after = unfolded(jnp.where(even, pair, other)) * has_after
    before = unfolded(jnp.where(even, other, pair)) * has_before
    x[0:rows] = x_ref[...]
    x[rows:] = jnp.concatenate([after, rest, rest, before], axis=0).astype(BF16)
    width = total.shape[1]
    for n in range(0, width, width // 3):
        part = slice(n, n + width // 3)
        for j in range(TAPS):
            product = rolled(jnp.dot(x[...], w1[j, :, part], preferred_element_type=F32), j)
            if j == 0:
                total[:, part] = product
            else:
                total[:, part] += product
        first_ref[0:rows, part] = jax.nn.gelu(total[0:rows, part]).astype(BF16)
    after = jax.nn.gelu(total[rows : rows + EDGE]) * has_after
    before = jax.nn.gelu(total[rows + EDGE :]) * has_before
    first_ref[rows:] = jnp.concatenate([after, before], axis=0).astype(BF16)


def second_kernel(first_ref, w2, wqkv, scale_hbm, *rest, heads, head, spread):
    hidden_ref, units, (total, scale_ref, sem) = rest[0], rest[1:-3], rest[-3:]
    scale_copy = pltpu.make_async_copy(scale_hbm, scale_ref, sem)
    scale_copy.start()
    rows = hidden_ref.shape[0]
    for j in range(TAPS):
        product = rolled(jnp.dot(first_ref[...], w2[j], preferred_element_type=F32), j)
        if j == 0:
            total[...] = product
        else:
            total[...] += product
    hidden_ref[...] = (first_ref[0:rows].astype(F32) + total[0:rows]).astype(BF16)
    scale_copy.wait()
    g = lax.axis_index("seq")
    project(hidden_ref, wqkv, scale_ref, units, g, range(len(units)), heads, head, spread)


def project(hidden_ref, wqkv, scale_ref, units, g, rounds, heads, head, spread):
    width = heads * head
    hidden = hidden_ref[...]
    for unit, r in zip(units, rounds):
        h = head_of(r, g, heads) if spread else r
        at = pl.multiple_of(h * head, head)
        weight = jnp.concatenate(
            [wqkv[:, pl.ds(part * width + at, head)] for part in range(3)], axis=1
        )
        projected = jnp.dot(hidden, weight, preferred_element_type=F32)
        q = head_rms(projected[:, :head]) * (scale_ref[h] / math.sqrt(head))
        unit[:, 0:head] = q.astype(BF16)
        unit[:, head : 2 * head] = head_rms(projected[:, head : 2 * head]).astype(BF16)
        unit[:, 2 * head :] = projected[:, 2 * head :].astype(BF16)


def third_kernel(hidden_ref, wqkv, scale_hbm, *rest, heads, head, spread):
    units, (scale_ref, sem) = rest[:-2], rest[-2:]
    scale_copy = pltpu.make_async_copy(scale_hbm, scale_ref, sem)
    scale_copy.start()
    scale_copy.wait()
    g = lax.axis_index("seq")
    rounds = range(heads - len(units), heads)
    project(hidden_ref, wqkv, scale_ref, units, g, rounds, heads, head, spread)


def head_of(r, g, heads):
    half = heads // 2
    side = g // heads
    return half * (side ^ 1 ^ (r // half)) + ((r % half) ^ (g % half))


def swaps(offset):
    count, batch_count = lax.axis_size("seq"), lax.axis_size("batch")
    pairs = []
    for g in range(count):
        for b in range(batch_count):
            to = ((g + offset) ^ 1) - offset
            target = (to, b) if 0 <= to < count else (g, b ^ 1 if b ^ 1 < batch_count else b)
            pairs.append((g * batch_count + b, target[0] * batch_count + target[1]))
    return pairs


def stem(block, conv_first, conv_second, qkv_weight, logit_scale, spread):
    rows, channels = block.shape
    width = conv_first.shape[2]
    heads = logit_scale.shape[0]
    head = qkv_weight.shape[1] // 3 // heads
    circle = rows + 2 * EDGE
    vmem = pl.BlockSpec(memory_space=pltpu.VMEM)
    hbm = pl.BlockSpec(memory_space=pltpu.HBM)
    shape = jax.ShapeDtypeStruct
    params = pltpu.CompilerParams(vmem_limit_bytes=24 * MIB)
    edge = shape((EDGE, channels // 2), BF16)
    to_pair, to_other = pl.pallas_call(
        edges_kernel,
        out_shape=[edge, edge],
        in_specs=[hbm] * 2,
        out_specs=[vmem] * 2,
        scratch_shapes=[pltpu.VMEM((TILE, channels), BF16)] * 2
        + [pltpu.SemaphoreType.DMA((2,))],
        compiler_params=params,
        name="edges",
    )(
        pltpu.with_memory_space_constraint(block, pltpu.HBM),
        pltpu.with_memory_space_constraint(conv_first, pltpu.HBM),
    )
    other = lax.ppermute(to_other, ("seq", "batch"), swaps(1))
    pair = lax.ppermute(to_pair, ("seq", "batch"), swaps(0))
    first = pl.pallas_call(
        functools.partial(first_kernel, count=lax.axis_size("seq")),
        out_shape=shape((circle, width), BF16),
        in_specs=[vmem] * 4,
        out_specs=vmem,
        scratch_shapes=[pltpu.VMEM((circle, channels), BF16), pltpu.VMEM((circle, width), F32)],
        compiler_params=params,
        name="first",
    )(block, other, pair, conv_first)
    half = 1
    fixed = dict(heads=heads, head=head, spread=spread)
    unit = shape((rows, 3 * head), BF16)
    scale_scratch = [pltpu.SMEM(logit_scale.shape, F32), pltpu.SemaphoreType.DMA]
    hidden, *units = pl.pallas_call(
        functools.partial(second_kernel, **fixed),
        out_shape=[shape((rows, width), BF16)] + [unit] * half,
        in_specs=[vmem] * 3 + [hbm],
        out_specs=[vmem] * (1 + half),
        scratch_shapes=[pltpu.VMEM((circle, width), F32)] + scale_scratch,
        compiler_params=params,
        name="second",
    )(first, conv_second, qkv_weight, logit_scale)
    units += pl.pallas_call(
        functools.partial(third_kernel, **fixed),
        out_shape=[unit] * (heads - half),
        in_specs=[vmem] * 2 + [hbm],
        out_specs=[vmem] * (heads - half),
        scratch_shapes=scale_scratch,
        compiler_params=pltpu.CompilerParams(vmem_limit_bytes=24 * MIB),
        name="third",
    )(hidden, qkv_weight, logit_scale)
    return [hidden, *units]


def scores_of(queries, keys):
    return lax.dot_general(
        queries, keys, (((1,), (1,)), ((), ())), preferred_element_type=F32
    )


def attend_units(queries, units, wide_sums=False):
    head = queries.shape[1]
    scores = [scores_of(queries, unit[:, head : 2 * head]) for unit in units]
    top = functools.reduce(jnp.maximum, [jnp.max(s, axis=1, keepdims=True) for s in scores])
    weights = [jnp.exp(s - top) for s in scores]
    values = jnp.concatenate([unit[:, 2 * head :] for unit in units], axis=0)
    if wide_sums:
        values = jnp.concatenate([values, jnp.ones_like(values)], axis=1)
    else:
        total = functools.reduce(jnp.add, [jnp.sum(w, axis=1, keepdims=True) for w in weights])
    weights = jnp.concatenate([w.astype(BF16) for w in weights], axis=1)
    mixed = jnp.dot(weights, values, preferred_element_type=F32)
    return (top, mixed[:, head:], mixed[:, :head]) if wide_sums else (top, total, mixed)


def attend_all_kernel(*refs, head, count):
    units, outs = refs[:-count], refs[-count:]
    for i in range(count):
        _, total, mixed = attend_units(units[i][:, 0:head], units)
        outs[i][...] = (mixed / total).astype(BF16)


def attend_some_kernel(*refs, head, count):
    units, (tops, totals, sums) = refs[:-3], refs[-3:]
    rows = units[0].shape[0]
    for i in range(count):
        part = slice(i * rows, (i + 1) * rows)
        top, total, sums[part] = attend_units(units[i][:, 0:head], units)
        tops[part] = jnp.broadcast_to(top, (rows, head))
        totals[part] = jnp.broadcast_to(total, (rows, head))


def attend_rest_kernel(*refs, head, count):
    units, (tops, totals, sums), outs = refs[: -3 - count], refs[-3 - count : -count], refs[-count:]
    rows = units[0].shape[0]
    for i in range(count):
        part = slice(i * rows, (i + 1) * rows)
        top, total, mixed = attend_units(units[i][:, 0:head], units[count:], wide_sums=True)
        top = jnp.broadcast_to(top, (rows, head))
        new_top = jnp.maximum(top, tops[part])
        old, new = jnp.exp(tops[part] - new_top), jnp.exp(top - new_top)
        total = totals[part] * old + total * new
        outs[i][...] = ((sums[part] * old + mixed * new) / total).astype(BF16)


def attend(kernel, count, out_shape, operands, name):
    vmem = pl.BlockSpec(memory_space=pltpu.VMEM)
    head = operands[0].shape[1] // 3
    return pl.pallas_call(
        functools.partial(kernel, head=head, count=count),
        out_shape=out_shape,
        in_specs=[vmem] * len(operands),
        out_specs=[vmem] * len(out_shape),
        compiler_params=pltpu.CompilerParams(vmem_limit_bytes=24 * MIB),
        name=name,
    )(*operands)


def attention(own, swap):
    rows, wide = own[0].shape
    shape = jax.ShapeDtypeStruct
    steps = [0, 1], [3, 2]
    result = [shape((rows, wide // 3), BF16)] * len(steps[0])
    partial = [shape((len(steps[0]) * rows, wide // 3), F32)] * 3
    other = [swap(unit) for unit in own]
    last = len(own) // 2 - 1
    queries = [own[r] for r in steps[0]]
    most = queries + [own[r] for r in steps[1]] + other[:last] + other[last + 1 :]
    part = attend(attend_some_kernel, len(queries), partial, most, "most")
    outs = attend(attend_rest_kernel, len(queries), result, [*queries, other[last], *part], "last")
    outs, own = lax.optimization_barrier((outs, own))
    queries = [own[r] for r in steps[1]]
    keys = queries + [own[r] for r in steps[0]] + other
    outs = outs + attend(attend_all_kernel, len(queries), result, keys, "near")
    return outs, steps[0] + steps[1]


def finish_kernel(hidden_ref, weight_ref, *rest, rounds, spread):
    mixed, out_ref = rest[:-1], rest[-1]
    g = lax.axis_index("seq")
    head = mixed[0].shape[1]
    heads = [head_of(r, g, len(mixed)) if spread else r for r in rounds]
    rows = [weight_ref[pl.ds(pl.multiple_of(h * head, head), head), :] for h in heads]
    attended = jnp.concatenate([part[...] for part in mixed], axis=1)
    projected = jnp.dot(attended, jnp.concatenate(rows, axis=0), preferred_element_type=F32)
    out_ref[...] = (hidden_ref[...].astype(F32) + projected).astype(out_ref.dtype)


def finish(hidden, out_weight, mixed, rounds, spread):
    vmem = pl.BlockSpec(memory_space=pltpu.VMEM)
    return pl.pallas_call(
        functools.partial(finish_kernel, rounds=rounds, spread=spread),
        out_shape=jax.ShapeDtypeStruct(hidden.shape, BF16),
        in_specs=[vmem] * (2 + len(mixed)),
        out_specs=vmem,
        compiler_params=pltpu.CompilerParams(vmem_limit_bytes=32 * MIB),
        name="finish",
    )(hidden, out_weight, *mixed)


def routes(seq_count, batch_count, heads):
    half = heads // 2
    rounds = []
    for r in range(heads):
        pairs = []
        for g in range(seq_count):
            for b in range(batch_count):
                h = head_of(r, g, heads)
                chip = heads * (h // half) + half * (b % 2 ^ h // half) + h % half
                far = h // half != g // heads
                core = (g // half + (h // half if far else 1 + g // heads)) % 2
                target = chip * batch_count + b - b % 2 + core
                pairs.append((g * batch_count + b, target))
        rounds.append(pairs)
    return rounds


def by_heads(sequence_input, conv_first, conv_second, qkv_weight, out_weight, logit_scale):
    heads = logit_scale.shape[0]
    count = lax.axis_size("seq")
    batch_count = lax.axis_size("batch")
    hidden, *units = stem(
        sequence_input, conv_first, conv_second, qkv_weight, logit_scale, True
    )
    both = ("seq", "batch")
    rounds = routes(count, batch_count, heads)
    own = [lax.ppermute(unit, both, pairs) for unit, pairs in zip(units, rounds)]
    cores = [(b, b ^ 1) for b in range(batch_count)]
    outs, order = attention(own, lambda unit: lax.ppermute(unit, "batch", cores))
    mixed = [
        lax.ppermute(out, both, [(target, source) for source, target in rounds[r]])
        for out, r in zip(outs, order)
    ]
    return finish(hidden, out_weight, mixed, order, True)


def by_gather(sequence_input, conv_first, conv_second, qkv_weight, out_weight, logit_scale):
    heads = logit_scale.shape[0]
    count = lax.axis_size("seq")
    hidden, *units = stem(
        sequence_input, conv_first, conv_second, qkv_weight, logit_scale, False
    )
    head = units[0].shape[1] // 3
    pairs = jnp.concatenate([unit[:, head:] for unit in units], axis=1)
    everywhere = lax.all_gather(pairs, "seq", axis=0, tiled=True)
    mixed = []
    for h in range(heads):
        at = 2 * h * head
        scores = lax.dot_general(
            units[h][:, :head],
            everywhere[:, at : at + head],
            (((1,), (1,)), ((), ())),
            preferred_element_type=F32,
        )
        weights = jnp.exp(scores - jnp.max(scores, axis=1, keepdims=True))
        denominators = jnp.sum(weights, axis=1, keepdims=True)
        out = jnp.dot(
            weights.astype(BF16),
            everywhere[:, at + head : at + 2 * head],
            preferred_element_type=F32,
        )
        mixed.append((out / denominators).astype(BF16))
    return finish(hidden, out_weight, mixed, range(heads), False)


def solution(mesh):
    def body(*args):
        heads = args[-1].shape[0]
        fits = heads == 4 and mesh.shape["seq"] == 2 * heads and mesh.shape["batch"] % 2 == 0
        return (by_heads if fits else by_gather)(*args)

    in_specs = (P(("batch", "seq"), None), P(), P(), P(), P(), P())
    out_specs = P(("batch", "seq"), None)
    return jax.shard_map(body, mesh=mesh, in_specs=in_specs, out_specs=out_specs, check_vma=False)
```

```python
import functools
import math

import jax
import jax.numpy as jnp
from jax import lax
from jax.experimental import pallas as pl
from jax.experimental.pallas import tpu as pltpu
from jax.sharding import PartitionSpec as P

F32 = jnp.float32
BF16 = jnp.bfloat16
EDGE = 8
REACH = 4
TILE = 16
TAPS = 5
MIB = 1 << 20


def head_rms(tensor):
    return tensor * lax.rsqrt(jnp.mean(tensor * tensor, axis=-1, keepdims=True) + 1e-06)


def edges_kernel(x_hbm, w1_hbm, to_pair, to_other, first, last, sems):
    rows = x_hbm.shape[0]
    copies = [
        pltpu.make_async_copy(x_hbm.at[pl.ds(0, TILE)], first, sems.at[0]),
        pltpu.make_async_copy(x_hbm.at[pl.ds(rows - TILE, TILE)], last, sems.at[1]),
    ]
    for copy in copies:
        copy.start()
    for copy in copies:
        copy.wait()
    even = lax.axis_index("seq") % 2 == 0
    begin = folded(first[...].astype(F32)[:REACH])
    end = folded(last[...].astype(F32)[TILE - REACH :])
    to_pair[...] = jnp.where(even, end, begin).astype(BF16)
    to_other[...] = jnp.where(even, begin, end).astype(BF16)


def folded(rows):
    half = rows.shape[1] // 2
    return jnp.concatenate([rows[:, :half], rows[:, half:]], axis=0)


def unfolded(rows):
    return jnp.concatenate([rows[:REACH], rows[REACH:]], axis=1)


def rolled(product, j):
    shift = (TAPS // 2 - j) % product.shape[0]
    return product if shift == 0 else pltpu.roll(product, shift, 0)


def first_kernel(x_ref, other_ref, pair_ref, w1, first_ref, x, total, *, count):
    rows = x_ref.shape[0]
    g = lax.axis_index("seq")
    even = g % 2 == 0
    has_before = (g > 0).astype(F32)
    has_after = (g < count - 1).astype(F32)
    pair, other = pair_ref[...].astype(F32), other_ref[...].astype(F32)
    rest = jnp.zeros((EDGE - REACH, x.shape[1]), F32)
    after = unfolded(jnp.where(even, pair, other)) * has_after
    before = unfolded(jnp.where(even, other, pair)) * has_before
    x[0:rows] = x_ref[...]
    x[rows:] = jnp.concatenate([after, rest, rest, before], axis=0).astype(BF16)
    width = total.shape[1]
    for n in range(0, width, width // 3):
        part = slice(n, n + width // 3)
        for j in range(TAPS):
            product = rolled(jnp.dot(x[...], w1[j, :, part], preferred_element_type=F32), j)
            if j == 0:
                total[:, part] = product
            else:
                total[:, part] += product
        first_ref[0:rows, part] = jax.nn.gelu(total[0:rows, part]).astype(BF16)
    after = jax.nn.gelu(total[rows : rows + EDGE]) * has_after
    before = jax.nn.gelu(total[rows + EDGE :]) * has_before
    first_ref[rows:] = jnp.concatenate([after, before], axis=0).astype(BF16)


def second_kernel(first_ref, w2, wqkv, scale_hbm, *rest, heads, head, spread):
    hidden_ref, units, (total, scale_ref, sem) = rest[0], rest[1:-3], rest[-3:]
    scale_copy = pltpu.make_async_copy(scale_hbm, scale_ref, sem)
    scale_copy.start()
    rows = hidden_ref.shape[0]
    width = total.shape[1]
    for n in range(0, width, width // 3):
        part = slice(n, n + width // 3)
        for j in range(TAPS):
            product = jnp.dot(first_ref[...], w2[j, :, part], preferred_element_type=F32)
            if j == 0:
                total[:, part] = rolled(product, j)
            else:
                total[:, part] += rolled(product, j)
        hidden = first_ref[0:rows, part].astype(F32) + total[0:rows, part]
        hidden_ref[:, part] = hidden.astype(BF16)
    scale_copy.wait()
    g = lax.axis_index("seq")
    project(hidden_ref, wqkv, scale_ref, units, g, range(len(units)), heads, head, spread)


def project(hidden_ref, wqkv, scale_ref, units, g, rounds, heads, head, spread):
    width = heads * head
    hidden = hidden_ref[...]
    for unit, r in zip(units, rounds):
        h = head_of(r, g, heads) if spread else r
        at = pl.multiple_of(h * head, head)
        weight = jnp.concatenate(
            [wqkv[:, pl.ds(part * width + at, head)] for part in range(3)], axis=1
        )
        projected = jnp.dot(hidden, weight, preferred_element_type=F32)
        q = head_rms(projected[:, :head]) * (scale_ref[h] / math.sqrt(head))
        unit[:, 0:head] = q.astype(BF16)
        unit[:, head : 2 * head] = head_rms(projected[:, head : 2 * head]).astype(BF16)
        unit[:, 2 * head :] = projected[:, 2 * head :].astype(BF16)


def third_kernel(hidden_ref, wqkv, scale_hbm, *rest, heads, head, spread):
    units, (scale_ref, sem) = rest[:-2], rest[-2:]
    scale_copy = pltpu.make_async_copy(scale_hbm, scale_ref, sem)
    scale_copy.start()
    scale_copy.wait()
    g = lax.axis_index("seq")
    rounds = range(heads - len(units), heads)
    project(hidden_ref, wqkv, scale_ref, units, g, rounds, heads, head, spread)


def head_of(r, g, heads):
    half = heads // 2
    side = g // heads
    return half * (side ^ 1 ^ (r // half)) + ((r % half) ^ (g % half))


def swaps(offset):
    count, batch_count = lax.axis_size("seq"), lax.axis_size("batch")
    pairs = []
    for g in range(count):
        for b in range(batch_count):
            to = ((g + offset) ^ 1) - offset
            target = (to, b) if 0 <= to < count else (g, b ^ 1 if b ^ 1 < batch_count else b)
            pairs.append((g * batch_count + b, target[0] * batch_count + target[1]))
    return pairs


def stem(block, conv_first, conv_second, qkv_weight, logit_scale, spread):
    rows, channels = block.shape
    width = conv_first.shape[2]
    heads = logit_scale.shape[0]
    head = qkv_weight.shape[1] // 3 // heads
    circle = rows + 2 * EDGE
    vmem = pl.BlockSpec(memory_space=pltpu.VMEM)
    hbm = pl.BlockSpec(memory_space=pltpu.HBM)
    shape = jax.ShapeDtypeStruct
    params = pltpu.CompilerParams(vmem_limit_bytes=24 * MIB)
    edge = shape((EDGE, channels // 2), BF16)
    to_pair, to_other = pl.pallas_call(
        edges_kernel,
        out_shape=[edge, edge],
        in_specs=[hbm] * 2,
        out_specs=[vmem] * 2,
        scratch_shapes=[pltpu.VMEM((TILE, channels), BF16)] * 2
        + [pltpu.SemaphoreType.DMA((2,))],
        compiler_params=params,
        name="edges",
    )(
        pltpu.with_memory_space_constraint(block, pltpu.HBM),
        pltpu.with_memory_space_constraint(conv_first, pltpu.HBM),
    )
    other = lax.ppermute(to_other, ("seq", "batch"), swaps(1))
    pair = lax.ppermute(to_pair, ("seq", "batch"), swaps(0))
    first = pl.pallas_call(
        functools.partial(first_kernel, count=lax.axis_size("seq")),
        out_shape=shape((circle, width), BF16),
        in_specs=[vmem] * 4,
        out_specs=vmem,
        scratch_shapes=[pltpu.VMEM((circle, channels), BF16), pltpu.VMEM((circle, width), F32)],
        compiler_params=params,
        name="first",
    )(block, other, pair, conv_first)
    half = 1
    fixed = dict(heads=heads, head=head, spread=spread)
    unit = shape((rows, 3 * head), BF16)
    scale_scratch = [pltpu.SMEM(logit_scale.shape, F32), pltpu.SemaphoreType.DMA]
    hidden, *units = pl.pallas_call(
        functools.partial(second_kernel, **fixed),
        out_shape=[shape((rows, width), BF16)] + [unit] * half,
        in_specs=[vmem] * 3 + [hbm],
        out_specs=[vmem] * (1 + half),
        scratch_shapes=[pltpu.VMEM((circle, width), F32)] + scale_scratch,
        compiler_params=params,
        name="second",
    )(first, conv_second, qkv_weight, logit_scale)
    units += pl.pallas_call(
        functools.partial(third_kernel, **fixed),
        out_shape=[unit] * (heads - half),
        in_specs=[vmem] * 2 + [hbm],
        out_specs=[vmem] * (heads - half),
        scratch_shapes=scale_scratch,
        compiler_params=pltpu.CompilerParams(vmem_limit_bytes=24 * MIB),
        name="third",
    )(hidden, qkv_weight, logit_scale)
    return [hidden, *units]


def scores_of(queries, keys):
    return lax.dot_general(
        queries, keys, (((1,), (1,)), ((), ())), preferred_element_type=F32
    )


def attend_units(queries, units, wide_sums=False):
    head = queries.shape[1]
    scores = [scores_of(queries, unit[:, head : 2 * head]) for unit in units]
    top = functools.reduce(jnp.maximum, [jnp.max(s, axis=1, keepdims=True) for s in scores])
    weights = [jnp.exp(s - top) for s in scores]
    values = jnp.concatenate([unit[:, 2 * head :] for unit in units], axis=0)
    if wide_sums:
        values = jnp.concatenate([values, jnp.ones_like(values)], axis=1)
    else:
        total = functools.reduce(jnp.add, [jnp.sum(w, axis=1, keepdims=True) for w in weights])
    weights = jnp.concatenate([w.astype(BF16) for w in weights], axis=1)
    mixed = jnp.dot(weights, values, preferred_element_type=F32)
    return (top, mixed[:, head:], mixed[:, :head]) if wide_sums else (top, total, mixed)


def attend_all_kernel(*refs, head, count):
    units, outs = refs[:-count], refs[-count:]
    for i in range(count):
        _, total, mixed = attend_units(units[i][:, 0:head], units)
        outs[i][...] = (mixed / total).astype(BF16)


def attend_some_kernel(*refs, head, count):
    units, (tops, totals, sums) = refs[:-3], refs[-3:]
    rows = units[0].shape[0]
    for i in range(count):
        part = slice(i * rows, (i + 1) * rows)
        top, total, sums[part] = attend_units(units[i][:, 0:head], units)
        tops[part] = jnp.broadcast_to(top, (rows, head))
        totals[part] = jnp.broadcast_to(total, (rows, head))


def attend_rest_kernel(*refs, head, count):
    units, (tops, totals, sums), outs = refs[: -3 - count], refs[-3 - count : -count], refs[-count:]
    rows = units[0].shape[0]
    for i in range(count):
        part = slice(i * rows, (i + 1) * rows)
        top, total, mixed = attend_units(units[i][:, 0:head], units[count:], wide_sums=True)
        top = jnp.broadcast_to(top, (rows, head))
        new_top = jnp.maximum(top, tops[part])
        old, new = jnp.exp(tops[part] - new_top), jnp.exp(top - new_top)
        total = totals[part] * old + total * new
        outs[i][...] = ((sums[part] * old + mixed * new) / total).astype(BF16)


def attend(kernel, count, out_shape, operands, name):
    vmem = pl.BlockSpec(memory_space=pltpu.VMEM)
    head = operands[0].shape[1] // 3
    return pl.pallas_call(
        functools.partial(kernel, head=head, count=count),
        out_shape=out_shape,
        in_specs=[vmem] * len(operands),
        out_specs=[vmem] * len(out_shape),
        compiler_params=pltpu.CompilerParams(vmem_limit_bytes=24 * MIB),
        name=name,
    )(*operands)


def attention(own, swap):
    rows, wide = own[0].shape
    shape = jax.ShapeDtypeStruct
    steps = [0, 1], [3, 2]
    result = [shape((rows, wide // 3), BF16)] * len(steps[0])
    partial = [shape((len(steps[0]) * rows, wide // 3), F32)] * 3
    other = [swap(unit) for unit in own]
    last = len(own) // 2 - 1
    queries = [own[r] for r in steps[0]]
    most = queries + [own[r] for r in steps[1]] + other[:last] + other[last + 1 :]
    part = attend(attend_some_kernel, len(queries), partial, most, "most")
    outs = attend(attend_rest_kernel, len(queries), result, [*queries, other[last], *part], "last")
    outs, own = lax.optimization_barrier((outs, own))
    queries = [own[r] for r in steps[1]]
    keys = queries + [own[r] for r in steps[0]] + other
    outs = outs + attend(attend_all_kernel, len(queries), result, keys, "near")
    return outs, steps[0] + steps[1]


def finish_kernel(hidden_ref, weight_ref, *rest, rounds, spread):
    mixed, out_ref = rest[:-1], rest[-1]
    g = lax.axis_index("seq")
    head = mixed[0].shape[1]
    heads = [head_of(r, g, len(mixed)) if spread else r for r in rounds]
    rows = [weight_ref[pl.ds(pl.multiple_of(h * head, head), head), :] for h in heads]
    attended = jnp.concatenate([part[...] for part in mixed], axis=1)
    projected = jnp.dot(attended, jnp.concatenate(rows, axis=0), preferred_element_type=F32)
    out_ref[...] = (hidden_ref[...].astype(F32) + projected).astype(out_ref.dtype)


def finish(hidden, out_weight, mixed, rounds, spread):
    vmem = pl.BlockSpec(memory_space=pltpu.VMEM)
    return pl.pallas_call(
        functools.partial(finish_kernel, rounds=rounds, spread=spread),
        out_shape=jax.ShapeDtypeStruct(hidden.shape, BF16),
        in_specs=[vmem] * (2 + len(mixed)),
        out_specs=vmem,
        compiler_params=pltpu.CompilerParams(vmem_limit_bytes=32 * MIB),
        name="finish",
    )(hidden, out_weight, *mixed)


def routes(seq_count, batch_count, heads):
    half = heads // 2
    rounds = []
    for r in range(heads):
        pairs = []
        for g in range(seq_count):
            for b in range(batch_count):
                h = head_of(r, g, heads)
                chip = heads * (h // half) + half * (b % 2 ^ h // half) + h % half
                far = h // half != g // heads
                core = (g // half + (h // half if far else 1 + g // heads)) % 2
                target = chip * batch_count + b - b % 2 + core
                pairs.append((g * batch_count + b, target))
        rounds.append(pairs)
    return rounds


def by_heads(sequence_input, conv_first, conv_second, qkv_weight, out_weight, logit_scale):
    heads = logit_scale.shape[0]
    count = lax.axis_size("seq")
    batch_count = lax.axis_size("batch")
    hidden, *units = stem(
        sequence_input, conv_first, conv_second, qkv_weight, logit_scale, True
    )
    both = ("seq", "batch")
    rounds = routes(count, batch_count, heads)
    own = [lax.ppermute(unit, both, pairs) for unit, pairs in zip(units, rounds)]
    cores = [(b, b ^ 1) for b in range(batch_count)]
    outs, order = attention(own, lambda unit: lax.ppermute(unit, "batch", cores))
    mixed = [
        lax.ppermute(out, both, [(target, source) for source, target in rounds[r]])
        for out, r in zip(outs, order)
    ]
    return finish(hidden, out_weight, mixed, order, True)


def by_gather(sequence_input, conv_first, conv_second, qkv_weight, out_weight, logit_scale):
    heads = logit_scale.shape[0]
    count = lax.axis_size("seq")
    hidden, *units = stem(
        sequence_input, conv_first, conv_second, qkv_weight, logit_scale, False
    )
    head = units[0].shape[1] // 3
    pairs = jnp.concatenate([unit[:, head:] for unit in units], axis=1)
    everywhere = lax.all_gather(pairs, "seq", axis=0, tiled=True)
    mixed = []
    for h in range(heads):
        at = 2 * h * head
        scores = lax.dot_general(
            units[h][:, :head],
            everywhere[:, at : at + head],
            (((1,), (1,)), ((), ())),
            preferred_element_type=F32,
        )
        weights = jnp.exp(scores - jnp.max(scores, axis=1, keepdims=True))
        denominators = jnp.sum(weights, axis=1, keepdims=True)
        out = jnp.dot(
            weights.astype(BF16),
            everywhere[:, at + head : at + 2 * head],
            preferred_element_type=F32,
        )
        mixed.append((out / denominators).astype(BF16))
    return finish(hidden, out_weight, mixed, range(heads), False)


def solution(mesh):
    def body(*args):
        heads = args[-1].shape[0]
        fits = heads == 4 and mesh.shape["seq"] == 2 * heads and mesh.shape["batch"] % 2 == 0
        return (by_heads if fits else by_gather)(*args)

    in_specs = (P(("batch", "seq"), None), P(), P(), P(), P(), P())
    out_specs = P(("batch", "seq"), None)
    return jax.shard_map(body, mesh=mesh, in_specs=in_specs, out_specs=out_specs, check_vma=False)
```
